128 devices in a mesh: lat: 16 (over x, y_lo, core), lon: 8 (over z, y_hi).
Axes of the slice: x: 4, y: 4 (y_hi: 2, y_lo: 2; y = y_hi * 2 + y_lo), z: 4, core: 2. Of those that a mesh axis runs over, the one named last changes fastest.
Arguments:
- ocean_state: float32 [100, 128, 1024], P(None, 'lat', 'lon'), may hold values from -6 to 6
- ocean_mask: int32 [128, 1024], P('lat', 'lon'), may hold values from 0 to 1, as said below
- cotangent: float32 [100, 128, 1024], P(None, 'lat', 'lon'), may hold values from -6 to 6
- encoder_weight: bfloat16 [200, 100], replicated, may hold values from -0.625 to 0.625
- encoder_bias: float32 [200], replicated, may hold values from -3 to 3
- depth_weight: float32 [200, 7, 7], replicated, may hold values from -0.875 to 0.875
- norm_gain: float32 [200], replicated, may hold values from 0.25 to 1.75
- up_weight: bfloat16 [800, 200], replicated, may hold values from -0.4375 to 0.4375
- down_weight: bfloat16 [200, 800], replicated, may hold values from -0.21875 to 0.21875
- decoder_weight: bfloat16 [100, 200], replicated, may hold values from -0.4375 to 0.4375
Outputs:
- state_grad: float32 [100, 128, 1024], P(None, 'lat', 'lon')
- up_grad: float32 [800, 200], replicated
- down_grad: float32 [200, 800], replicated
- depth_grad: float32 [200, 7, 7], replicated
The draws below stay inside these ranges and needn't reach their ends.
Inputs may be any that keep to these rules, and one draw needn't show every extreme that they name: `ocean_mask`: 1 marks an ocean cell, 0 a land cell.
All inputs are finite; a program needn't handle non-finite values.
Results may differ from the reference program's by a relative error of at most 0.012.
Values may be sent and summed in bfloat16 or wider, within the bound.
A program may use at most 128 MiB of HBM per device.

```python
import math
import jax
import jax.numpy as jnp
from jax import lax

LEVELS = 100
MODEL_WIDTH = 200
HIDDEN_SIZE = 800
BAND_ROWS = 8
LAT_CELLS = 128
LON_CELLS = 1024


def draw_ocean_mask(key, part):
    key = jax.random.fold_in(key, 11)
    center_key, drift_key, width_key, jitter_key, flip_key = jax.random.split(key, 5)
    masses = 3
    latitude = jnp.arange(LAT_CELLS, dtype=jnp.int32)
    longitude = jnp.arange(LON_CELLS, dtype=jnp.int32)
    centers = jax.random.randint(center_key, (masses,), 0, LON_CELLS, dtype=jnp.int32)
    drifts = jax.random.randint(drift_key, (masses,), -3, 4, dtype=jnp.int32)
    widths = jax.random.randint(width_key, (masses,), 30, 80, dtype=jnp.int32)
    jitter = jax.random.randint(jitter_key, (masses, LAT_CELLS), 0, 16, dtype=jnp.int32)
    moved = (centers[:, None] + latitude[None, :] * drifts[:, None] // 4) % LON_CELLS
    half_width = LON_CELLS * (widths[:, None] + jitter) // 600 + 1
    offset = jnp.abs(longitude[None, None, :] - moved[:, :, None])
    beside_all = jnp.minimum(offset, LON_CELLS - offset)
    land = jnp.any(beside_all < half_width[:, :, None], axis=0)
    flips = jax.random.randint(flip_key, (LAT_CELLS, LON_CELLS), 0, 20, dtype=jnp.int32) == 0
    land = jnp.logical_xor(land, flips)
    return jnp.where(land, 0, 1).astype(jnp.int32)


def steps_of(rng, extent, cuts, least, largest):
    loudness, own = 1.0, jax.random.fold_in(rng, 6)
    for position, blocks in cuts:
        draws = jnp.exp(jax.random.uniform(jax.random.fold_in(own, position), (blocks,), jnp.float32, least / len(cuts), largest / len(cuts)))
        loudness = loudness * jnp.repeat(draws, extent[position] // blocks).reshape([-1 if axis == position else 1 for axis in range(len(extent))])
    return loudness


def gaussian(key, extent, scale, limit, cuts=(), held_as=jnp.bfloat16):
    drawn = scale * jax.random.normal(key, extent, jnp.float32)
    if cuts:
        drawn = drawn * steps_of(key, extent, cuts, -0.22, 0.18)
    return jnp.clip(drawn, -limit, limit).astype(held_as)


def setup_inputs(seed: int = 0) -> dict:
    key_list = jax.random.split(jax.random.key(seed), 11)
    ocean_state = gaussian(key_list[0], (LEVELS, LAT_CELLS, LON_CELLS), 1.0, 6.0, ((1, 16), (2, 8)), jnp.float32)
    ocean_mask = draw_ocean_mask(jax.random.fold_in(key_list[10], 71), 0)
    cotangent = gaussian(key_list[2], (LEVELS, LAT_CELLS, LON_CELLS), 1.0, 6.0, ((1, 16), (2, 8)), jnp.float32)
    encoder_weight = gaussian(key_list[3], (MODEL_WIDTH, LEVELS), LEVELS ** -0.5, 0.625)
    encoder_bias = gaussian(key_list[4], (MODEL_WIDTH,), 0.5, 3.0, (), jnp.float32)
    depth_weight = gaussian(key_list[5], (MODEL_WIDTH, 7, 7), 49 ** -0.5, 0.875, (), jnp.float32)
    norm_gain = jnp.clip(1.0 + 0.15 * jax.random.normal(key_list[6], (MODEL_WIDTH,), jnp.float32), 0.25, 1.75)
    up_weight = gaussian(key_list[7], (HIDDEN_SIZE, MODEL_WIDTH), MODEL_WIDTH ** -0.5, 0.4375)
    down_weight = gaussian(key_list[8], (MODEL_WIDTH, HIDDEN_SIZE), HIDDEN_SIZE ** -0.5, 0.21875)
    decoder_weight = gaussian(key_list[9], (LEVELS, MODEL_WIDTH), MODEL_WIDTH ** -0.5, 0.4375)
    return {"ocean_state": ocean_state, "ocean_mask": ocean_mask, "cotangent": cotangent, "encoder_weight": encoder_weight, "encoder_bias": encoder_bias, "depth_weight": depth_weight, "norm_gain": norm_gain, "up_weight": up_weight, "down_weight": down_weight, "decoder_weight": decoder_weight}


EPSILON = 1e-06
GELU_SCALE = 0.7978845608028654
GELU_CUBE = 0.044715

def gelu_value(preact):
    tangent = jnp.tanh(GELU_SCALE * (preact + GELU_CUBE * preact * preact * preact))
    return 0.5 * preact * (1.0 + tangent)

def gelu_slope(preact):
    tangent = jnp.tanh(GELU_SCALE * (preact + GELU_CUBE * preact * preact * preact))
    return 0.5 * (1.0 + tangent) + 0.5 * preact * (1.0 - tangent * tangent) * GELU_SCALE * (1.0 + 3.0 * GELU_CUBE * preact * preact)

def project(weight, features):
    flat_in = features.reshape(features.shape[0], -1)
    result = jnp.dot(weight, flat_in, preferred_element_type=jnp.float32)
    return result.reshape((weight.shape[0],) + features.shape[1:])

def outer_sum(left, right):
    return lax.dot_general(left, right, (((1,), (1,)), ((), ())), preferred_element_type=jnp.float32)

def encode(ocean_state, encoder_weight, encoder_bias, inside_rows):
    projected = project(encoder_weight, ocean_state.astype(jnp.bfloat16))
    return ((projected + encoder_bias[:, None, None]) * inside_rows).astype(jnp.bfloat16)

def depth_conv(padded, depth_weight):
    row_count = padded.shape[1] - 6
    col_count = padded.shape[2] - 6
    result = jnp.zeros((padded.shape[0], row_count, col_count), jnp.float32)
    for row_shift in range(7):
        for col_shift in range(7):
            window = padded[:, row_shift:row_shift + row_count, col_shift:col_shift + col_count].astype(jnp.float32)
            result = result + depth_weight[:, row_shift, col_shift][:, None, None] * window
    return result

def depth_reverse(padded, depth_weight):
    row_count = padded.shape[1] - 6
    col_count = padded.shape[2] - 6
    result = jnp.zeros((padded.shape[0], row_count, col_count), jnp.float32)
    for row_shift in range(7):
        for col_shift in range(7):
            window = padded[:, 6 - row_shift:6 - row_shift + row_count, 6 - col_shift:6 - col_shift + col_count]
            result = result + depth_weight[:, row_shift, col_shift][:, None, None] * window
    return result

def depth_weight_grad(slope, padded):
    row_count = slope.shape[1]
    col_count = slope.shape[2]
    columns = []
    for row_shift in range(7):
        for col_shift in range(7):
            window = padded[:, row_shift:row_shift + row_count, col_shift:col_shift + col_count].astype(jnp.float32)
            columns.append(lax.optimization_barrier(jnp.sum(slope * window, axis=(1, 2))))
    return jnp.stack(columns, axis=1).reshape(slope.shape[0], 7, 7)

def normalize(convolved):
    centre = convolved - lax.optimization_barrier(jnp.mean(convolved, axis=0, keepdims=True))
    inverse_std = lax.rsqrt(lax.optimization_barrier(jnp.mean(centre * centre, axis=0, keepdims=True)) + EPSILON)
    return (centre * inverse_std, inverse_std)

def expand_forward(normed, ocean_float, up_weight, down_weight):
    preact = jnp.dot(up_weight, normed, preferred_element_type=jnp.float32)
    activated = gelu_value(preact).astype(jnp.bfloat16)
    return ocean_float * jnp.dot(down_weight, activated, preferred_element_type=jnp.float32)

def expand_reverse(normed, ocean_float, grad_join, up_weight, down_weight):
    preact = jnp.dot(up_weight, normed, preferred_element_type=jnp.float32)
    activated = gelu_value(preact).astype(jnp.bfloat16)
    grad_branch = (ocean_float * grad_join).astype(jnp.bfloat16)
    grad_act = jnp.dot(down_weight.T, grad_branch, preferred_element_type=jnp.float32)
    grad_pre = (grad_act * gelu_slope(preact)).astype(jnp.bfloat16)
    grad_norm = jnp.dot(up_weight.T, grad_pre, preferred_element_type=jnp.float32)
    return (grad_norm, outer_sum(grad_pre, normed), outer_sum(grad_branch, activated))

def to_bands(features):
    channels, height, breadth = features.shape
    return jnp.moveaxis(features.reshape(channels, height // BAND_ROWS, BAND_ROWS * breadth), 1, 0)

def from_bands(blocks, height):
    return jnp.moveaxis(blocks, 0, 1).reshape(blocks.shape[1], height, -1)

def expand_whole(normed, ocean_float, up_weight, down_weight):

    def per_band(pieces):
        return expand_forward(pieces[0], pieces[1], up_weight, down_weight)
    blocks = lax.map(per_band, (to_bands(normed), to_bands(ocean_float[None])))
    return from_bands(blocks, normed.shape[1])

def reverse_whole(normed, ocean_float, grad_join, up_weight, down_weight):

    def per_band(pieces):
        return expand_reverse(pieces[0], pieces[1], pieces[2], up_weight, down_weight)
    grad_norm, up_terms, down_terms = lax.map(per_band, (to_bands(normed), to_bands(ocean_float[None]), to_bands(grad_join)))
    return (from_bands(grad_norm, normed.shape[1]), lax.optimization_barrier(jnp.sum(up_terms, axis=0)), lax.optimization_barrier(jnp.sum(down_terms, axis=0)))

def pad_whole(features, margin):
    row_padded = jnp.pad(features, ((0, 0), (margin, margin), (0, 0)))
    return jnp.concatenate([row_padded[:, :, -margin:], row_padded, row_padded[:, :, :margin]], axis=2)

def finish(convolved, features, ocean_state, ocean_float, weights):
    encoder_weight, encoder_bias, depth_weight, norm_gain, up_weight, down_weight, decoder_weight = weights
    standard, inverse_std = normalize(convolved)
    normed = (standard * norm_gain[:, None, None]).astype(jnp.bfloat16)
    branch = expand_whole(normed, ocean_float, up_weight, down_weight)
    joined = (features.astype(jnp.float32) + branch).astype(jnp.bfloat16)
    return ocean_state + ocean_float * project(decoder_weight, joined)

def reverse_step(padded, ocean_float, upstream, weights):
    encoder_weight, encoder_bias, depth_weight, norm_gain, up_weight, down_weight, decoder_weight = weights
    convolved = depth_conv(padded, depth_weight)
    standard, inverse_std = normalize(convolved)
    normed = (standard * norm_gain[:, None, None]).astype(jnp.bfloat16)
    scaled = (ocean_float * upstream).astype(jnp.bfloat16)
    grad_join = project(decoder_weight.T, scaled)
    grad_norm, up_term, down_term = reverse_whole(normed, ocean_float, grad_join, up_weight, down_weight)
    grad_hat = grad_norm * norm_gain[:, None, None]
    grad_conv = inverse_std * (grad_hat - lax.optimization_barrier(jnp.mean(grad_hat, axis=0, keepdims=True)) - standard * lax.optimization_barrier(jnp.mean(grad_hat * standard, axis=0, keepdims=True)))
    depth_term = depth_weight_grad(grad_conv, padded)
    grad_field = grad_join + depth_reverse(pad_whole(grad_conv, 3), depth_weight)
    grad_input = grad_field.astype(jnp.bfloat16)
    return ((up_term, down_term, depth_term), upstream + project(encoder_weight.T, grad_input))

def reference(ocean_state, ocean_mask, cotangent, encoder_weight, encoder_bias, depth_weight, norm_gain, up_weight, down_weight, decoder_weight):
    ocean_float = ocean_mask.astype(jnp.float32)
    weights = (encoder_weight, encoder_bias, depth_weight, norm_gain, up_weight, down_weight, decoder_weight)
    unit_scale = jnp.float32(1.0)
    features = encode(ocean_state, encoder_weight, encoder_bias, unit_scale)
    first_padded = pad_whole(features, 3)
    middle = finish(depth_conv(first_padded, depth_weight), features, ocean_state, ocean_float, weights)
    middle_padded = pad_whole(encode(middle, encoder_weight, encoder_bias, unit_scale), 3)
    late_terms, grad_middle = reverse_step(middle_padded, ocean_float, cotangent, weights)
    early_terms, state_grad = reverse_step(first_padded, ocean_float, grad_middle, weights)
    grad_scale = 1.0 / math.sqrt(LAT_CELLS * LON_CELLS)
    return (state_grad, (late_terms[0] + early_terms[0]) * grad_scale, (late_terms[1] + early_terms[1]) * grad_scale, (late_terms[2] + early_terms[2]) * grad_scale)
```

```python
import math

import jax
import jax.numpy as jnp
import numpy as np
from jax import lax
from jax.experimental import pallas as pl
from jax.experimental.pallas import tpu as pltpu
from jax.sharding import PartitionSpec as P

EPSILON = 1e-06
GELU_SCALE = 0.7978845608028654
GELU_CUBE = 0.044715
MESH = pl.DeviceIdType.MESH
F32 = jnp.float32
BF16 = jnp.bfloat16
LEVELS = 100
WIDTH = 200
HIDDEN = 800
ROWS = 8
COLS = 128
CHUNKS = 4
SPAN = 256
BLOCKS = WIDTH // 8

STEPS = ((1, 0), (-1, 0), (0, 1), (0, -1), (1, 1), (1, -1), (-1, 1), (-1, -1))
LINES = {2: (16, 16, 32), 3: (80, 80, 32), 4: (48, 0, 16), 5: (112, 64, 16), 6: (0, 48, 16), 7: (64, 112, 16)}


def edge_tables():
    pack = np.zeros((ROWS * COLS, 128), np.float32)
    spread = np.zeros((128, 14 * COLS), np.float32)
    for side in range(2):
        for first, rows, sent, filled in ((0, 3, 0, 0), (16, 8, 0, 3), (48, 3, 5, 11)):
            for q in range(3 * rows):
                row, k = q // 3, q % 3
                line = 64 * side + first + q
                pack[COLS * (sent + row) + (k if side else 125 + k), line] = 1.0
                spread[line, COLS * (filled + row) + (k if side else 125 + k)] = 1.0
    return pack.astype(jnp.bfloat16), spread.astype(jnp.bfloat16)


def dot(a, b):
    return jnp.dot(a, b, preferred_element_type=F32)


def dot_nt(a, b):
    return lax.dot_general(a, b, (((1,), (1,)), ((), ())), preferred_element_type=F32)


def gelu_parts(p):
    square = p * p
    half = 0.5 * jnp.tanh(p * (GELU_SCALE + (GELU_SCALE * GELU_CUBE) * square)) + 0.5
    value = p * half
    slope = half + value * (1.0 - half) * (2.0 * GELU_SCALE + (6.0 * GELU_SCALE * GELU_CUBE) * square)
    return value, slope


def rows_of(value):
    return value[:, :COLS], value[:, COLS:]


def pair(ref, k):
    return jnp.concatenate([ref[2 * k], ref[2 * k + 1]], axis=1)


def main_kernel(
    state, mask, cot, encw, params, upw, downw, decw, pack, spread,
    out, up_out, down_out, depth_out,
    taps, pad_one, side_one, pad_two, side_two, pad_g, side_g, grad, conv, std_one, std_two, inv_one, inv_two,
    act_one, slope_one, normed_one, normed_two, join, grad_mid, depth_acc,
    upt, downt, dect, enct, own, edge_rows, line_out, line_in, send_sem, recv_sem,
):
    lat, lon = lax.axis_index("lat"), lax.axis_index("lon")
    lats, lons = lax.axis_size("lat"), lax.axis_size("lon")
    has_north, has_south = lat > 0, lat < lats - 1
    north, south = lat - 1, lat + 1
    east, west = lax.rem(lon + 1, lons), lax.rem(lon + lons - 1, lons)
    lat_of = {0: lat, 1: south, -1: north}
    lon_of = {0: lon, 1: east, -1: west}

    def when_lat(step, run):
        if step == 0:
            run()
        elif step > 0:
            pl.when(has_south)(run)
        else:
            pl.when(has_north)(run)

    barrier = pltpu.get_barrier_semaphore()
    for step_lat, step_lon in STEPS:
        when_lat(step_lat, lambda a=step_lat, b=step_lon: pl.semaphore_signal(
            barrier, inc=1, device_id=(lat_of[a], lon_of[b]), device_id_type=MESH))

    def copy_of(turn, m):
        if m == 0:
            src, dst = own.at[turn, pl.ds(5, 3)], edge_rows.at[turn, 0]
        elif m == 1:
            src, dst = own.at[turn, pl.ds(0, 3)], edge_rows.at[turn, 1]
        else:
            first, filled, count = LINES[m]
            src, dst = line_out.at[turn, pl.ds(first, count)], line_in.at[turn, pl.ds(filled, count)]
        return pltpu.make_async_remote_copy(
            src_ref=src, dst_ref=dst, send_sem=send_sem.at[turn, m], recv_sem=recv_sem.at[turn, m],
            device_id=(lat_of[STEPS[m][0]], lon_of[STEPS[m][1]]), device_id_type=MESH)

    def send_halo(turn):
        for m in (0, 1):
            when_lat(STEPS[m][0], lambda m=m: copy_of(turn, m).start())
        flat = jnp.concatenate([own[turn, r] for r in range(ROWS)], axis=1)
        picked = dot(flat, pack[...])
        picked = jnp.concatenate([picked, jnp.zeros((48, 128), F32)], axis=0)
        line_out[turn] = picked.T.astype(BF16)
        for m in range(2, 8):
            when_lat(STEPS[m][0], lambda m=m: copy_of(turn, m).start())

    def take_halo(turn, pad, side):
        for m in range(8):
            when_lat(-STEPS[m][0], lambda m=m: copy_of(turn, m).wait_recv())
        for r in range(3):
            pad[r] = edge_rows[turn, 0, r].astype(F32)[:WIDTH]
            pad[11 + r] = edge_rows[turn, 1, r].astype(F32)[:WIDTH]
        lines = line_in[turn].astype(F32).T[:WIDTH].astype(BF16)
        wide = dot(lines, spread[...])
        for r in range(14):
            side[r] = wide[:, COLS * r : COLS * (r + 1)]

    def keep(turn, k, value, pad):
        rounded = value.astype(BF16)
        again = rounded.astype(F32)
        filled = jnp.concatenate([value, jnp.zeros((8, SPAN), F32)], axis=0).astype(BF16)
        for q in range(2):
            pad[3 + 2 * k + q] = again[:, COLS * q : COLS * (q + 1)]
            own[turn, 2 * k + q] = filled[:, COLS * q : COLS * (q + 1)]
        return again

    lane = lax.broadcasted_iota(jnp.int32, (14, 8, COLS), 2)

    def shifted(main, edge, s):
        if s == 0:
            return main
        if s > 0:
            return pltpu.roll(jnp.where(lane < s, edge, main), COLS - s, 2)
        return pltpu.roll(jnp.where(lane >= COLS + s, edge, main), -s, 2)

    def depthwise(pad, side, target, adjoint):
        def block(b, carry):
            at = pl.ds(pl.multiple_of(8 * b, 8), 8)
            main, edge = pad[:, at, :], side[:, at, :]
            total = jnp.zeros((ROWS, 8, COLS), F32)
            for j in range(7):
                moved = shifted(main, edge, 3 - j if adjoint else j - 3)
                for i in range(7):
                    first = 6 - i if adjoint else i
                    total = total + taps[7 * i + j, at, :][None] * moved[first : first + ROWS]
            target[:, at, :] = total
            return carry
        lax.fori_loop(0, BLOCKS, block, 0)

    def depth_terms(pad, side, fresh):
        def block(b, carry):
            at = pl.ds(pl.multiple_of(8 * b, 8), 8)
            main, edge, slope = pad[:, at, :], side[:, at, :], grad[:, at, :]
            for j in range(7):
                moved = shifted(main, edge, j - 3)
                for i in range(7):
                    term = jnp.sum(slope * moved[i : i + ROWS], axis=0)
                    if fresh:
                        depth_acc[7 * i + j, at, :] = term
                    else:
                        depth_acc[7 * i + j, at, :] += term
            return carry
        lax.fori_loop(0, BLOCKS, block, 0)

    def over_chunks(body):
        lax.fori_loop(0, CHUNKS, lambda k, c: (body(k), c)[1], 0)

    def mask_of(k):
        both = jnp.concatenate([mask[pl.ds(2 * k, 1), :], mask[pl.ds(2 * k + 1, 1), :]], axis=1)
        return both.astype(F32)

    def levels_of(ref, k):
        return jnp.concatenate(
            [ref[pl.ds(2 * k + q, LEVELS, stride=ROWS), :] for q in range(2)], axis=1)

    bias = params[:, 49:50]
    gain = params[:, 50:51]

    def encode(k, value, turn, pad):
        keep(turn, k, dot(encw[...], value.astype(BF16)) + bias, pad)

    over_chunks(lambda k: encode(k, levels_of(state, k), 0, pad_one))

    def ends(turn):
        @pl.when(jnp.logical_not(has_north))
        def _():
            edge_rows[turn, 0] = jnp.zeros_like(edge_rows[turn, 0])
            for part in (0, 64):
                line_in[turn, pl.ds(part, 16)] = jnp.zeros((16, SPAN), BF16)

        @pl.when(jnp.logical_not(has_south))
        def _():
            edge_rows[turn, 1] = jnp.zeros_like(edge_rows[turn, 1])
            for part in (48, 112):
                line_in[turn, pl.ds(part, 16)] = jnp.zeros((16, SPAN), BF16)

    peers = 2 + 3 * jnp.minimum(lat, 1) + 3 * jnp.minimum(lats - 1 - lat, 1)
    pl.semaphore_wait(barrier, peers)
    send_halo(0)

    for turn in range(4):
        ends(turn)
    for t in range(49):
        taps[t] = jnp.broadcast_to(params[:, t : t + 1], (WIDTH, COLS))
    upt[...] = upw[...].astype(F32).T.astype(BF16)
    downt[...] = downw[...].astype(F32).T.astype(BF16)
    dect[...] = decw[...].astype(F32).T.astype(BF16)
    enct[...] = encw[...].astype(F32).T.astype(BF16)

    take_halo(0, pad_one, side_one)
    depthwise(pad_one, side_one, conv, False)

    def normalize(k, std, inv, normed):
        value = pair(conv, k)
        centre = value - jnp.sum(value, axis=0, keepdims=True) * (1.0 / WIDTH)
        inverse = lax.rsqrt(jnp.sum(centre * centre, axis=0, keepdims=True) * (1.0 / WIDTH) + EPSILON)
        standard = centre * inverse
        std[2 * k], std[2 * k + 1] = rows_of(standard)
        inv[k] = jnp.broadcast_to(inverse, (8, SPAN))
        result = (standard * gain).astype(BF16)
        normed[k] = result
        return result

    def forward(k):
        ocean = mask_of(k)
        preact = dot(upw[...], normalize(k, std_one, inv_one, normed_one))
        value, slope = gelu_parts(preact)
        value = value.astype(BF16)
        act_one[k] = value
        slope_one[k] = slope.astype(BF16)
        features = jnp.concatenate([pad_one[3 + 2 * k], pad_one[4 + 2 * k]], axis=1)
        joined = (features + ocean * dot(downw[...], value)).astype(BF16)
        middle = levels_of(state, k) + ocean * dot(decw[...], joined)
        encode(k, middle, 1, pad_two)

    over_chunks(forward)
    send_halo(1)
    take_halo(1, pad_two, side_two)
    depthwise(pad_two, side_two, conv, False)

    def reverse(k, turn, upstream, normed, value, slope, std, inv, fresh):
        ocean = mask_of(k)
        grad_join = dot(dect[...], (ocean * upstream).astype(BF16))
        join[k] = grad_join
        grad_branch = (ocean * grad_join).astype(BF16)
        grad_pre = (dot(downt[...], grad_branch) * slope).astype(BF16)
        grad_norm = dot(upt[...], grad_pre)
        up_term = dot_nt(grad_pre, normed)
        down_term = dot_nt(value, grad_branch)
        if fresh:
            @pl.when(k == 0)
            def _():
                up_out[...] = up_term
                down_out[...] = down_term

            @pl.when(k > 0)
            def _():
                up_out[...] += up_term
                down_out[...] += down_term
        else:
            up_out[...] += up_term
            down_out[...] += down_term
        standard = pair(std, k)
        grad_hat = grad_norm * gain
        first = jnp.sum(grad_hat, axis=0, keepdims=True) * (1.0 / WIDTH)
        second = jnp.sum(grad_hat * standard, axis=0, keepdims=True) * (1.0 / WIDTH)
        result = inv[k][0:1] * (grad_hat - first - standard * second)
        grad[2 * k], grad[2 * k + 1] = rows_of(result)
        keep(turn, k, result, pad_g)

    def late(k):
        normed = normalize(k, std_two, inv_two, normed_two)
        value, slope = gelu_parts(dot(upw[...], normed))
        reverse(k, 2, levels_of(cot, k), normed, value.astype(BF16), slope, std_two, inv_two, True)

    over_chunks(late)
    send_halo(2)
    depth_terms(pad_two, side_two, True)
    take_halo(2, pad_g, side_g)
    depthwise(pad_g, side_g, conv, True)

    def early(k):
        grad_input = (join[k] + pair(conv, k)).astype(BF16)
        upstream = levels_of(cot, k) + dot(enct[...], grad_input)
        grad_mid[k] = upstream
        reverse(k, 3, upstream, normed_one[k], act_one[k], slope_one[k].astype(F32), std_one, inv_one, False)

    over_chunks(early)
    send_halo(3)
    depth_terms(pad_one, side_one, False)
    take_halo(3, pad_g, side_g)
    depthwise(pad_g, side_g, conv, True)

    def last(k):
        grad_input = (join[k] + pair(conv, k)).astype(BF16)
        result = grad_mid[k] + dot(enct[...], grad_input)
        for q in range(2):
            out[pl.ds(2 * k + q, LEVELS, stride=ROWS), :] = result[:, COLS * q : COLS * (q + 1)]

    over_chunks(last)
    column = lax.broadcasted_iota(jnp.int32, (WIDTH, COLS), 1)
    picked = jnp.zeros((WIDTH, COLS), F32)
    for t in range(49):
        picked = jnp.where(column == t, jnp.sum(depth_acc[t], axis=1, keepdims=True), picked)
    depth_out[...] = picked
    for turn in range(4):
        for m in range(8):
            when_lat(STEPS[m][0], lambda m=m: copy_of(turn, m).wait_send())


def main_call(*operands):
    vmem = pl.BlockSpec(memory_space=pltpu.VMEM)
    padded = pltpu.VMEM((14, WIDTH, COLS), F32)
    plane = pltpu.VMEM((ROWS, WIDTH, COLS), F32)
    return pl.pallas_call(
        main_kernel,
        out_shape=[
            jax.ShapeDtypeStruct((LEVELS * ROWS, COLS), F32),
            jax.ShapeDtypeStruct((HIDDEN, WIDTH), F32),
            jax.ShapeDtypeStruct((HIDDEN, WIDTH), F32),
            jax.ShapeDtypeStruct((WIDTH, COLS), F32),
        ],
        in_specs=[vmem] * len(operands),
        out_specs=[vmem] * 4,
        scratch_shapes=[
            pltpu.VMEM((49, WIDTH, COLS), F32),
            padded, padded, padded, padded, padded, padded,
            plane, plane, plane, plane,
            pltpu.VMEM((CHUNKS, 8, SPAN), F32),
            pltpu.VMEM((CHUNKS, 8, SPAN), F32),
            pltpu.VMEM((CHUNKS, HIDDEN, SPAN), BF16),
            pltpu.VMEM((CHUNKS, HIDDEN, SPAN), BF16),
            pltpu.VMEM((CHUNKS, WIDTH, SPAN), BF16),
            pltpu.VMEM((CHUNKS, WIDTH, SPAN), BF16),
            pltpu.VMEM((CHUNKS, WIDTH, SPAN), F32),
            pltpu.VMEM((CHUNKS, LEVELS, SPAN), F32),
            pltpu.VMEM((49, WIDTH, COLS), F32),
            pltpu.VMEM((WIDTH, HIDDEN), BF16),
            pltpu.VMEM((HIDDEN, WIDTH), BF16),
            pltpu.VMEM((WIDTH, LEVELS), BF16),
            pltpu.VMEM((LEVELS, WIDTH), BF16),
            pltpu.VMEM((4, ROWS, 208, COLS), BF16),
            pltpu.VMEM((4, 2, 3, 208, COLS), BF16),
            pltpu.VMEM((4, 128, SPAN), BF16),
            pltpu.VMEM((4, 128, SPAN), BF16),
            pltpu.SemaphoreType.DMA((4, 8)),
            pltpu.SemaphoreType.DMA((4, 8)),
        ],
        compiler_params=pltpu.CompilerParams(
            collective_id=0, has_side_effects=True, vmem_limit_bytes=58 * 1024 * 1024),
    )(*operands)


def per_device(
    ocean_state, ocean_mask, cotangent, encoder_weight, encoder_bias, depth_weight,
    norm_gain, up_weight, down_weight, decoder_weight,
):
    total_rows = ROWS * lax.axis_size("lat")
    total_cols = COLS * lax.axis_size("lon")
    params = jnp.concatenate(
        [depth_weight.reshape(WIDTH, 49), encoder_bias[:, None], norm_gain[:, None], jnp.zeros((WIDTH, 77), F32)],
        axis=1)
    pack, spread = edge_tables()
    state_grad, up_sum, down_sum, depth_sum = main_call(
        ocean_state.reshape(LEVELS * ROWS, COLS), ocean_mask, cotangent.reshape(LEVELS * ROWS, COLS),
        encoder_weight, params, up_weight, down_weight, decoder_weight,
        jnp.asarray(pack), jnp.asarray(spread))
    joined = jnp.concatenate([up_sum, down_sum, jnp.pad(depth_sum, ((0, 0), (0, WIDTH - COLS)))], axis=0)
    summed = lax.psum(joined, ("lat", "lon")) * (1.0 / math.sqrt(total_rows * total_cols))
    return (
        state_grad.reshape(ocean_state.shape),
        summed[:HIDDEN],
        summed[HIDDEN : 2 * HIDDEN].T,
        summed[2 * HIDDEN :, :49].reshape(WIDTH, 7, 7),
    )


def solution(mesh):
    return jax.shard_map(
        per_device,
        mesh=mesh,
        in_specs=(
            P(None, "lat", "lon"), P("lat", "lon"), P(None, "lat", "lon"),
            P(), P(), P(), P(), P(), P(), P(),
        ),
        out_specs=(P(None, "lat", "lon"), P(), P(), P()),
        check_vma=False,
    )
```

```python
import functools
import math

import jax
import jax.numpy as jnp
import numpy as np
from jax import lax
from jax.experimental import pallas as pl
from jax.experimental.pallas import tpu as pltpu
from jax.sharding import PartitionSpec as P

EPSILON = 1e-06
GELU_SCALE = 0.7978845608028654
GELU_CUBE = 0.044715
MESH = pl.DeviceIdType.MESH
F32 = jnp.float32
BF16 = jnp.bfloat16
LEVELS = 100
WIDTH = 200
HIDDEN = 800
ROWS = 8
COLS = 128
CHUNKS = 4
SPAN = 256
BLOCKS = WIDTH // 8

STEPS = ((1, 0), (-1, 0), (0, 1), (0, -1), (1, 1), (1, -1), (-1, 1), (-1, -1))
LINES = {2: (16, 16, 32), 3: (80, 80, 32), 4: (48, 0, 16), 5: (112, 64, 16), 6: (0, 48, 16), 7: (64, 112, 16)}


def edge_tables():
    pack = np.zeros((ROWS * COLS, 128), np.float32)
    spread = np.zeros((128, 14 * COLS), np.float32)
    for side in range(2):
        for first, rows, sent, filled in ((0, 3, 0, 0), (16, 8, 0, 3), (48, 3, 5, 11)):
            for q in range(3 * rows):
                row, k = q // 3, q % 3
                line = 64 * side + first + q
                pack[COLS * (sent + row) + (k if side else 125 + k), line] = 1.0
                spread[line, COLS * (filled + row) + (k if side else 125 + k)] = 1.0
    return pack.astype(jnp.bfloat16), spread.astype(jnp.bfloat16)


def dot(a, b):
    return jnp.dot(a, b, preferred_element_type=F32)


def dot_nt(a, b):
    return lax.dot_general(a, b, (((1,), (1,)), ((), ())), preferred_element_type=F32)


def gelu_parts(p):
    square = p * p
    half = 0.5 * jnp.tanh(p * (GELU_SCALE + (GELU_SCALE * GELU_CUBE) * square)) + 0.5
    value = p * half
    slope = half + value * (1.0 - half) * (2.0 * GELU_SCALE + (6.0 * GELU_SCALE * GELU_CUBE) * square)
    return value, slope


def rows_of(value):
    return value[:, :COLS], value[:, COLS:]


def pair(ref, k):
    return jnp.concatenate([ref[2 * k], ref[2 * k + 1]], axis=1)


def main_kernel(
    scale, state, mask, cot, encw, bias_in, depth_in, gain_in, upt, downw, dect, pack, spread,
    out, up_out, down_out, depth_out,
    taps, pad_one, side_one, pad_two, side_two, pad_g, side_g, grad, conv, std_one, std_two, inv_one, inv_two,
    act_one, slope_one, normed_one, normed_two, join, grad_mid, depth_acc,
    upw, downt, decw, enct, own, edge_rows, line_out, line_in, send_sem, recv_sem,
    tall, params, sums, half_out, half_in, quarter_out, quarter_in, slot_sum, slot_out, slot_in, slot_done, gathered,
    depth_own, depth_got, depth_mid, depth_peer, depth_all, sum_send, sum_recv,
):
    lat, lon = lax.axis_index("lat"), lax.axis_index("lon")
    lats, lons = lax.axis_size("lat"), lax.axis_size("lon")
    has_north, has_south = lat > 0, lat < lats - 1
    north, south = lat - 1, lat + 1
    east, west = lax.rem(lon + 1, lons), lax.rem(lon + lons - 1, lons)
    x_at, core = lat // 4, lax.rem(lat, 2)
    member = lon // 2 * 4 + lax.rem(lon, 2) * 2 + lax.rem(lat // 2, 2)

    def core_peer():
        return (lat + 1 - 2 * core, lon)

    def line_peer(d):
        return (lax.rem(x_at + d, 4) * 4 + lax.rem(lat, 4), lon)

    def chip_peer(d):
        flip, step = d // 4, d % 4
        side = 1 - core if flip else core
        return (lax.rem(x_at + step, 4) * 4 + lax.rem(lat // 2, 2) * 2 + side, lon)

    def member_at(d):
        return lax.rem(member + d, 16)

    def plane_peer(d):
        other = member_at(d)
        z_at, y_at = other // 4, lax.rem(other, 4)
        return (x_at * 4 + lax.rem(y_at, 2) * 2 + core, z_at * 2 + y_at // 2)

    lat_of = {0: lat, 1: south, -1: north}
    lon_of = {0: lon, 1: east, -1: west}

    def when_lat(step, run):
        if step == 0:
            run()
        elif step > 0:
            pl.when(has_south)(run)
        else:
            pl.when(has_north)(run)

    barrier = pltpu.get_barrier_semaphore()
    for step_lat, step_lon in STEPS:
        when_lat(step_lat, lambda a=step_lat, b=step_lon: pl.semaphore_signal(
            barrier, inc=1, device_id=(lat_of[a], lon_of[b]), device_id_type=MESH))

    for peer in [chip_peer(d) for d in range(1, 8)] + [plane_peer(d) for d in range(1, 16)]:
        pl.semaphore_signal(barrier, inc=1, device_id=peer, device_id_type=MESH)

    def copy_of(turn, m):
        if m == 0:
            src, dst = own.at[turn, pl.ds(5, 3)], edge_rows.at[turn, 0]
        elif m == 1:
            src, dst = own.at[turn, pl.ds(0, 3)], edge_rows.at[turn, 1]
        else:
            first, filled, count = LINES[m]
            src, dst = line_out.at[turn, pl.ds(first, count)], line_in.at[turn, pl.ds(filled, count)]
        return pltpu.make_async_remote_copy(
            src_ref=src, dst_ref=dst, send_sem=send_sem.at[turn, m], recv_sem=recv_sem.at[turn, m],
            device_id=(lat_of[STEPS[m][0]], lon_of[STEPS[m][1]]), device_id_type=MESH)

    def send_halo(turn):
        for m in (0, 1):
            when_lat(STEPS[m][0], lambda m=m: copy_of(turn, m).start())
        flat = jnp.concatenate([own[turn, r] for r in range(ROWS)], axis=1)
        picked = dot(flat, pack[...])
        picked = jnp.concatenate([picked, jnp.zeros((48, 128), F32)], axis=0)
        line_out[turn] = picked.T.astype(BF16)
        for m in range(2, 8):
            when_lat(STEPS[m][0], lambda m=m: copy_of(turn, m).start())

    def take_halo(turn, pad, side):
        for m in range(8):
            when_lat(-STEPS[m][0], lambda m=m: copy_of(turn, m).wait_recv())
        for r in range(3):
            pad[r] = edge_rows[turn, 0, r].astype(F32)[:WIDTH]
            pad[11 + r] = edge_rows[turn, 1, r].astype(F32)[:WIDTH]
        lines = line_in[turn].astype(F32).T[:WIDTH].astype(BF16)
        wide = dot(lines, spread[...])
        for r in range(14):
            side[r] = wide[:, COLS * r : COLS * (r + 1)]

    def keep(turn, k, value, pad):
        rounded = value.astype(BF16)
        again = rounded.astype(F32)
        filled = jnp.concatenate([value, jnp.zeros((8, SPAN), F32)], axis=0).astype(BF16)
        for q in range(2):
            pad[3 + 2 * k + q] = again[:, COLS * q : COLS * (q + 1)]
            own[turn, 2 * k + q] = filled[:, COLS * q : COLS * (q + 1)]
        return again

    lane = lax.broadcasted_iota(jnp.int32, (14, 8, COLS), 2)

    def shifted(main, edge, s):
        if s == 0:
            return main
        if s > 0:
            return pltpu.roll(jnp.where(lane < s, edge, main), COLS - s, 2)
        return pltpu.roll(jnp.where(lane >= COLS + s, edge, main), -s, 2)

    def depthwise(pad, side, target, adjoint, first_block=0, last_block=BLOCKS):
        def block(b, carry):
            at = pl.ds(pl.multiple_of(8 * b, 8), 8)
            main, edge = pad[:, at, :], side[:, at, :]
            total = jnp.zeros((ROWS, 8, COLS), F32)
            for j in range(7):
                moved = shifted(main, edge, 3 - j if adjoint else j - 3)
                for i in range(7):
                    first = 6 - i if adjoint else i
                    total = total + taps[7 * i + j, at, :][None] * moved[first : first + ROWS]
            target[:, at, :] = total
            return carry
        lax.fori_loop(first_block, last_block, block, 0)

    def depth_terms(pad, side, fresh, first_block=0, last_block=BLOCKS):
        def block(b, carry):
            at = pl.ds(pl.multiple_of(8 * b, 8), 8)
            main, edge, slope = pad[:, at, :], side[:, at, :], grad[:, at, :]
            for j in range(7):
                moved = shifted(main, edge, j - 3)
                for i in range(7):
                    term = jnp.sum(slope * moved[i : i + ROWS], axis=0)
                    if fresh:
                        depth_acc[7 * i + j, at, :] = term
                    else:
                        depth_acc[7 * i + j, at, :] += term
            return carry
        lax.fori_loop(first_block, last_block, block, 0)

    def over_chunks(body):
        lax.fori_loop(0, CHUNKS, lambda k, c: (body(k), c)[1], 0)

    def mask_of(k):
        both = jnp.concatenate([mask[pl.ds(2 * k, 1), :], mask[pl.ds(2 * k + 1, 1), :]], axis=1)
        return both.astype(F32)

    def levels_of(ref, k):
        return jnp.concatenate(
            [ref[pl.ds(2 * k + q, LEVELS, stride=ROWS), :] for q in range(2)], axis=1)

    tall[...] = jnp.zeros_like(tall)
    for i in range(7):
        tall[7 * i : 7 * i + 7, :WIDTH] = depth_in[i]
    tall[49:50, :WIDTH] = bias_in[...]
    tall[50:51, :WIDTH] = gain_in[...]
    params[...] = tall[...].T[:WIDTH]
    bias = params[:, 49:50]
    gain = params[:, 50:51]

    def encode(k, value, turn, pad):
        keep(turn, k, dot(encw[...], value.astype(BF16)) + bias, pad)

    over_chunks(lambda k: encode(k, levels_of(state, k), 0, pad_one))

    def ends(turn):
        @pl.when(jnp.logical_not(has_north))
        def _():
            edge_rows[turn, 0] = jnp.zeros_like(edge_rows[turn, 0])
            for part in (0, 64):
                line_in[turn, pl.ds(part, 16)] = jnp.zeros((16, SPAN), BF16)

        @pl.when(jnp.logical_not(has_south))
        def _():
            edge_rows[turn, 1] = jnp.zeros_like(edge_rows[turn, 1])
            for part in (48, 112):
                line_in[turn, pl.ds(part, 16)] = jnp.zeros((16, SPAN), BF16)

    peers = 24 + 3 * jnp.minimum(lat, 1) + 3 * jnp.minimum(lats - 1 - lat, 1)
    pl.semaphore_wait(barrier, peers)
    send_halo(0)

    for turn in range(4):
        ends(turn)
    for t in range(49):
        taps[t] = jnp.broadcast_to(params[:, t : t + 1], (WIDTH, COLS))
    upw[...] = upt[...].astype(F32).T.astype(BF16)
    sums[...] = jnp.zeros_like(sums)
    downt[...] = downw[...].astype(F32).T.astype(BF16)
    decw[...] = dect[...].astype(F32).T.astype(BF16)
    enct[...] = encw[...].astype(F32).T.astype(BF16)

    take_halo(0, pad_one, side_one)
    depthwise(pad_one, side_one, conv, False)

    def normalize(k, std, inv, normed):
        value = pair(conv, k)
        centre = value - jnp.sum(value, axis=0, keepdims=True) * (1.0 / WIDTH)
        inverse = lax.rsqrt(jnp.sum(centre * centre, axis=0, keepdims=True) * (1.0 / WIDTH) + EPSILON)
        standard = centre * inverse
        std[2 * k], std[2 * k + 1] = rows_of(standard)
        inv[k] = jnp.broadcast_to(inverse, (8, SPAN))
        result = (standard * gain).astype(BF16)
        normed[k] = result
        return result

    def forward(k):
        ocean = mask_of(k)
        preact = dot(upw[...], normalize(k, std_one, inv_one, normed_one))
        value, slope = gelu_parts(preact)
        value = value.astype(BF16)
        act_one[k] = value
        slope_one[k] = slope.astype(BF16)
        features = jnp.concatenate([pad_one[3 + 2 * k], pad_one[4 + 2 * k]], axis=1)
        joined = (features + ocean * dot(downw[...], value)).astype(BF16)
        middle = levels_of(state, k) + ocean * dot(decw[...], joined)
        encode(k, middle, 1, pad_two)

    over_chunks(forward)
    send_halo(1)
    take_halo(1, pad_two, side_two)
    depthwise(pad_two, side_two, conv, False)

    def reverse(k, turn, upstream, normed, value, slope, std, inv):
        ocean = mask_of(k)
        grad_join = dot(dect[...], (ocean * upstream).astype(BF16))
        join[k] = grad_join
        grad_branch = (ocean * grad_join).astype(BF16)
        grad_pre = (dot(downt[...], grad_branch) * slope).astype(BF16)
        grad_norm = dot(upt[...], grad_pre)
        for which, term in ((0, dot_nt(normed, grad_pre)), (1, dot_nt(grad_branch, value))):
            for part in range(3):
                sums[which, part, :WIDTH, :] += term[:, SPAN * part : SPAN * (part + 1)]
            sums[which, 3, :WIDTH, : HIDDEN - 3 * SPAN] += term[:, 3 * SPAN :]
        standard = pair(std, k)
        grad_hat = grad_norm * gain
        first = jnp.sum(grad_hat, axis=0, keepdims=True) * (1.0 / WIDTH)
        second = jnp.sum(grad_hat * standard, axis=0, keepdims=True) * (1.0 / WIDTH)
        result = inv[k][0:1] * (grad_hat - first - standard * second)
        grad[2 * k], grad[2 * k + 1] = rows_of(result)
        keep(turn, k, result, pad_g)

    def late(k):
        normed = normalize(k, std_two, inv_two, normed_two)
        value, slope = gelu_parts(dot(upw[...], normed))
        reverse(k, 2, levels_of(cot, k), normed, value.astype(BF16), slope, std_two, inv_two)

    over_chunks(late)
    send_halo(2)
    depth_terms(pad_two, side_two, True)
    take_halo(2, pad_g, side_g)
    depthwise(pad_g, side_g, conv, True)

    def early(k):
        grad_input = (join[k] + pair(conv, k)).astype(BF16)
        upstream = levels_of(cot, k) + dot(enct[...], grad_input)
        grad_mid[k] = upstream
        reverse(k, 3, upstream, normed_one[k], act_one[k], slope_one[k].astype(F32), std_one, inv_one)

    over_chunks(early)
    send_halo(3)

    def remote(src, dst, slot, peer):
        return pltpu.make_async_remote_copy(
            src_ref=src, dst_ref=dst, send_sem=sum_send.at[slot], recv_sem=sum_recv.at[slot],
            device_id=peer, device_id_type=MESH)

    half = remote(half_out, half_in, 0, core_peer())
    quarters = [
        remote(quarter_out.at[lax.rem(x_at + d, 4)], quarter_in.at[d - 1], d, line_peer(d)) for d in range(1, 4)]

    def slot_copy(d):
        other = jnp.minimum(member_at(d), 12)
        rows = pl.ds(pl.multiple_of(16 * other, 16), 16)
        return remote(slot_out.at[rows], slot_in.at[d - 1], 3 + d, plane_peer(d))

    def done_copy(d):
        return remote(slot_done, gathered.at[core, x_at, mine], 18 + d, plane_peer(d))

    def line_copy(d):
        return remote(gathered.at[core, x_at], gathered.at[core, x_at], 33 + d, line_peer(d))

    back = remote(gathered.at[core], gathered.at[core], 37, core_peer())
    mine = pl.ds(pl.multiple_of(16 * jnp.minimum(member, 12), 16), 16)

    def depth_copy(d):
        return remote(depth_own.at[member_at(d)], depth_got.at[d - 1], 37 + d, plane_peer(d))

    def peer_copy(d):
        return remote(depth_mid, depth_peer.at[d - 1], 52 + d, chip_peer(d))

    def spread_copy(d):
        return remote(depth_all.at[member], depth_all.at[member], 59 + d, plane_peer(d))

    def owner(index):
        return lambda run: pl.when(index < 13)(run)

    half_out[...] = sums[1 - core].astype(BF16)
    half.start()
    depth_terms(pad_one, side_one, False, 0, 9)

    half.wait_recv()
    for part in range(4):
        quarter_out[part] = (sums[core, part] + half_in[part].astype(F32)).astype(BF16)
    for copy in quarters:
        copy.start()
    slot_sum[...] = sums[core, x_at] + half_in[x_at].astype(F32)
    depth_terms(pad_one, side_one, False, 9, BLOCKS)

    for copy in quarters:
        copy.wait_recv()
    slot_sum[...] = slot_sum[...] + (
        quarter_in[0].astype(F32) + quarter_in[1].astype(F32) + quarter_in[2].astype(F32))
    slot_out[...] = slot_sum[...].astype(BF16)
    for d in range(1, 16):
        owner(member_at(d))(lambda d=d: slot_copy(d).start())

    column = lax.broadcasted_iota(jnp.int32, (WIDTH, COLS), 1)
    picked = jnp.zeros((WIDTH, COLS), F32)
    for t in range(49):
        picked = jnp.where(column == t, jnp.sum(depth_acc[t], axis=1, keepdims=True), picked)
    turned = jnp.concatenate([picked, jnp.zeros((56, COLS), F32)], axis=0).T
    for piece in range(16):
        depth_own[piece] = turned[
            8 * (piece // 2) : 8 * (piece // 2) + 8, COLS * (piece % 2) : COLS * (piece % 2) + COLS]
    for d in range(1, 16):
        depth_copy(d).start()

    take_halo(3, pad_g, side_g)
    depthwise(pad_g, side_g, conv, True, 0, 8)

    @pl.when(member < 13)
    def _():
        total = slot_sum[mine, :]
        for d in range(1, 16):
            slot_copy(d).wait_recv()
            total = total + slot_in[d - 1].astype(F32)
        total = (total * scale).astype(BF16)
        slot_done[...] = total
        gathered[core, x_at, mine, :] = total
        for d in range(1, 16):
            done_copy(d).start()

    total = depth_own[member]
    for d in range(1, 16):
        depth_copy(d).wait_recv()
        total = total + depth_got[d - 1]
    depth_mid[...] = total
    for d in range(1, 8):
        peer_copy(d).start()
    depthwise(pad_g, side_g, conv, True, 8, 16)

    for d in range(1, 16):
        owner(member_at(16 - d))(lambda d=d: done_copy(d).wait_recv())
    for d in range(1, 4):
        line_copy(d).start()
    total = depth_mid[...]
    for d in range(1, 8):
        peer_copy(d).wait_recv()
        total = total + depth_peer[d - 1]
    depth_all[member] = total * scale
    for d in range(1, 16):
        spread_copy(d).start()
    depthwise(pad_g, side_g, conv, True, 16, BLOCKS)

    for d in range(1, 4):
        line_copy(d).wait_recv()
    back.start()

    def last(k):
        grad_input = (join[k] + pair(conv, k)).astype(BF16)
        result = grad_mid[k] + dot(enct[...], grad_input)
        for q in range(2):
            out[pl.ds(2 * k + q, LEVELS, stride=ROWS), :] = result[:, COLS * q : COLS * (q + 1)]

    over_chunks(last)
    for d in range(1, 16):
        spread_copy(d).wait_recv()
    for piece in range(16):
        row, left = 8 * (piece // 2), COLS * (piece % 2)
        width = min(COLS, WIDTH - left)
        for t in range(row, min(row + 8, 49)):
            depth_out[t // 7, t % 7 : t % 7 + 1, left : left + width] = depth_all[piece, t - row : t - row + 1, :width]
    back.wait_recv()
    for which, target in ((0, up_out), (1, down_out)):
        for part in range(4):
            left = SPAN * part
            width = min(SPAN, HIDDEN - left)
            target[:, left : left + width] = gathered[which, part].astype(F32)[:WIDTH, :width]

    half.wait_send()
    for copy in quarters:
        copy.wait_send()
    back.wait_send()
    for d in range(1, 4):
        line_copy(d).wait_send()
    for d in range(1, 8):
        peer_copy(d).wait_send()
    for d in range(1, 16):
        owner(member_at(d))(lambda d=d: slot_copy(d).wait_send())
        owner(member)(lambda d=d: done_copy(d).wait_send())
        depth_copy(d).wait_send()
        spread_copy(d).wait_send()
    for turn in range(4):
        for m in range(8):
            when_lat(STEPS[m][0], lambda m=m: copy_of(turn, m).wait_send())


def main_call(scale, *operands):
    vmem = pl.BlockSpec(memory_space=pltpu.VMEM)
    padded = pltpu.VMEM((14, WIDTH, COLS), F32)
    plane = pltpu.VMEM((ROWS, WIDTH, COLS), F32)
    tile = (8, COLS)
    return pl.pallas_call(
        functools.partial(main_kernel, scale),
        out_shape=[
            jax.ShapeDtypeStruct((LEVELS * ROWS, COLS), F32),
            jax.ShapeDtypeStruct((WIDTH, HIDDEN), F32),
            jax.ShapeDtypeStruct((WIDTH, HIDDEN), F32),
            jax.ShapeDtypeStruct((7, 7, WIDTH), F32),
        ],
        in_specs=[vmem] * len(operands),
        out_specs=[vmem] * 4,
        scratch_shapes=[
            pltpu.VMEM((49, WIDTH, COLS), F32),
            padded, padded, padded, padded, padded, padded,
            plane, plane, plane, plane,
            pltpu.VMEM((CHUNKS, 8, SPAN), F32),
            pltpu.VMEM((CHUNKS, 8, SPAN), F32),
            pltpu.VMEM((CHUNKS, HIDDEN, SPAN), BF16),
            pltpu.VMEM((CHUNKS, HIDDEN, SPAN), BF16),
            pltpu.VMEM((CHUNKS, WIDTH, SPAN), BF16),
            pltpu.VMEM((CHUNKS, WIDTH, SPAN), BF16),
            pltpu.VMEM((CHUNKS, WIDTH, SPAN), F32),
            pltpu.VMEM((CHUNKS, LEVELS, SPAN), F32),
            pltpu.VMEM((49, WIDTH, COLS), F32),
            pltpu.VMEM((HIDDEN, WIDTH), BF16),
            pltpu.VMEM((HIDDEN, WIDTH), BF16),
            pltpu.VMEM((LEVELS, WIDTH), BF16),
            pltpu.VMEM((LEVELS, WIDTH), BF16),
            pltpu.VMEM((4, ROWS, 208, COLS), BF16),
            pltpu.VMEM((4, 2, 3, 208, COLS), BF16),
            pltpu.VMEM((4, 128, SPAN), BF16),
            pltpu.VMEM((4, 128, SPAN), BF16),
            pltpu.SemaphoreType.DMA((4, 8)),
            pltpu.SemaphoreType.DMA((4, 8)),
            pltpu.VMEM((128, SPAN), F32),
            pltpu.VMEM((WIDTH, COLS), F32),
            pltpu.VMEM((2, 4, 208, SPAN), F32),
            pltpu.VMEM((4, 208, SPAN), BF16),
            pltpu.VMEM((4, 208, SPAN), BF16),
            pltpu.VMEM((4, 208, SPAN), BF16),
            pltpu.VMEM((3, 208, SPAN), BF16),
            pltpu.VMEM((208, SPAN), F32),
            pltpu.VMEM((208, SPAN), BF16),
            pltpu.VMEM((15, 16, SPAN), BF16),
            pltpu.VMEM((16, SPAN), BF16),
            pltpu.VMEM((2, 4, 208, SPAN), BF16),
            pltpu.VMEM((16,) + tile, F32),
            pltpu.VMEM((15,) + tile, F32),
            pltpu.VMEM(tile, F32),
            pltpu.VMEM((7,) + tile, F32),
            pltpu.VMEM((16,) + tile, F32),
            pltpu.SemaphoreType.DMA((75,)),
            pltpu.SemaphoreType.DMA((75,)),
        ],
        compiler_params=pltpu.CompilerParams(
            collective_id=0, has_side_effects=True, vmem_limit_bytes=58 * 1024 * 1024),
    )(*operands)


def per_device(
    ocean_state, ocean_mask, cotangent, encoder_weight, encoder_bias, depth_weight,
    norm_gain, up_weight, down_weight, decoder_weight,
):
    cells = ROWS * lax.axis_size("lat") * COLS * lax.axis_size("lon")
    pack, spread = edge_tables()
    state_grad, up_sum, down_sum, depth_sum = main_call(
        1.0 / math.sqrt(cells),
        ocean_state.reshape(LEVELS * ROWS, COLS), ocean_mask, cotangent.reshape(LEVELS * ROWS, COLS),
        encoder_weight, encoder_bias[None, :], jnp.transpose(depth_weight, (1, 2, 0)), norm_gain[None, :],
        up_weight.T, down_weight, decoder_weight.T, jnp.asarray(pack), jnp.asarray(spread))
    return (
        state_grad.reshape(ocean_state.shape),
        up_sum.T,
        down_sum,
        jnp.transpose(depth_sum, (2, 0, 1)),
    )


def solution(mesh):
    return jax.shard_map(
        per_device,
        mesh=mesh,
        in_specs=(
            P(None, "lat", "lon"), P("lat", "lon"), P(None, "lat", "lon"),
            P(), P(), P(), P(), P(), P(), P(),
        ),
        out_specs=(P(None, "lat", "lon"), P(), P(), P()),
        check_vma=False,
    )
```

```python
import functools
import math

import jax
import jax.numpy as jnp
import numpy as np
from jax import lax
from jax.experimental import pallas as pl
from jax.experimental.pallas import tpu as pltpu
from jax.sharding import PartitionSpec as P

EPSILON = 1e-06
GELU_SCALE = 0.7978845608028654
GELU_CUBE = 0.044715
MESH = pl.DeviceIdType.MESH
F32 = jnp.float32
BF16 = jnp.bfloat16
LEVELS = 100
WIDTH = 200
HIDDEN = 800
ROWS = 8
COLS = 128
CHUNKS = 4
SPAN = 256
BLOCKS = WIDTH // 8

STEPS = ((-1, 0), (1, 0), (1, 0), (-1, 0), (0, 1), (0, -1), (1, 1), (1, -1), (-1, 1), (-1, -1))
BANDS = ((0, 1, 0, 2), (6, 0, 1, 2), (5, 0, 0, 1), (2, 1, 2, 1))
LINES = {4: (16, 16, 32), 5: (80, 80, 32), 6: (48, 0, 16), 7: (112, 64, 16), 8: (0, 48, 16), 9: (64, 112, 16)}
ORDER = (0, 3, 2, 1)
BAND_OF = {0: 0, 3: 1, 2: 2, 1: 3}
MEETS = tuple((0, x, k, k - x) for x in range(3) for k in range(x, 3)) + tuple(
    (1, x, k, 6 + k - x) for x in range(3) for k in range(x + 1))


def edge_tables():
    pack = np.zeros((ROWS * COLS, 128), np.float32)
    spread = np.zeros((CHUNKS, 128, SPAN), np.float32)
    for side in range(2):
        for k in range(3):
            column = k if side else 125 + k
            for first, step, sent, rows in ((0, 4, 0, 3), (16, 8, 0, 8), (48, 4, 5, 3)):
                for r in range(rows):
                    pack[COLS * (sent + r) + column, 64 * side + first + step * k + r] = 1.0
            for y in range(ROWS):
                column = 125 + k if side else k
                for part in (0, 48):
                    spread[y // 2, part + 24 * side + 8 * k + y, COLS * (y % 2) + column] = 1.0
    return pack.astype(jnp.bfloat16), spread.astype(jnp.bfloat16)


def dot(a, b):
    return jnp.dot(a, b, preferred_element_type=F32)


def dot_nt(a, b):
    return lax.dot_general(a, b, (((1,), (1,)), ((), ())), preferred_element_type=F32)


def gelu_parts(p):
    square = p * p
    half = 0.5 * jnp.tanh(p * (GELU_SCALE + (GELU_SCALE * GELU_CUBE) * square)) + 0.5
    value = p * half
    slope = half + value * (1.0 - half) * (2.0 * GELU_SCALE + (6.0 * GELU_SCALE * GELU_CUBE) * square)
    return value, slope


def rows_of(value):
    return value[:, :COLS], value[:, COLS:]


def pair(ref, k):
    return jnp.concatenate([ref[2 * k], ref[2 * k + 1]], axis=1)


def main_kernel(
    scale, state, mask, cot, encw, bias_in, depth_in, gain_in, upt, downw, dect, pack, spread,
    out, gathered, depth_out,
    taps, pad_one, pad_two, pad_g, grad, conv, std_one, std_two, inv_one, inv_two,
    act_one, slope_one, normed_one, normed_two, join, grad_mid, depth_acc,
    upw, downt, decw, enct, own, edge_rows, line_out, line_in, send_sem, recv_sem,
    tall, params, sums, half_out, half_in, quarter_out, quarter_in, slot_sum, slot_out, slot_in, slot_done,
    depth_own, depth_got, depth_mid, depth_peer, depth_all, sum_send, sum_recv,
    edges, fix, edge_terms,
):
    lat, lon = lax.axis_index("lat"), lax.axis_index("lon")
    lats, lons = lax.axis_size("lat"), lax.axis_size("lon")
    has_north, has_south = lat > 0, lat < lats - 1
    north, south = lat - 1, lat + 1
    east, west = lax.rem(lon + 1, lons), lax.rem(lon + lons - 1, lons)
    x_at, core = lat // 4, lax.rem(lat, 2)
    member = lon // 2 * 4 + lax.rem(lon, 2) * 2 + lax.rem(lat // 2, 2)

    def core_peer():
        return (lat + 1 - 2 * core, lon)

    def line_peer(d):
        return (lax.rem(x_at + d, 4) * 4 + lax.rem(lat, 4), lon)

    def chip_peer(d):
        flip, step = d // 4, d % 4
        side = 1 - core if flip else core
        return (lax.rem(x_at + step, 4) * 4 + lax.rem(lat // 2, 2) * 2 + side, lon)

    def member_at(d):
        return lax.rem(member + d, 16)

    def plane_peer(d):
        other = member_at(d)
        z_at, y_at = other // 4, lax.rem(other, 4)
        return (x_at * 4 + lax.rem(y_at, 2) * 2 + core, z_at * 2 + y_at // 2)

    lat_of = {0: lat, 1: south, -1: north}
    lon_of = {0: lon, 1: east, -1: west}

    def when_lat(step, run):
        if step == 0:
            run()
        elif step > 0:
            pl.when(has_south)(run)
        else:
            pl.when(has_north)(run)

    barrier = pltpu.get_barrier_semaphore()
    for step_lat, step_lon in STEPS[2:]:
        when_lat(step_lat, lambda a=step_lat, b=step_lon: pl.semaphore_signal(
            barrier, inc=1, device_id=(lat_of[a], lon_of[b]), device_id_type=MESH))

    for peer in [chip_peer(d) for d in range(1, 8)] + [plane_peer(d) for d in range(1, 16)]:
        pl.semaphore_signal(barrier, inc=1, device_id=peer, device_id_type=MESH)

    def copy_of(turn, m):
        if m < 4:
            first, side, filled, count = BANDS[m]
            src = own.at[turn, pl.ds(first, count)]
            dst = edge_rows.at[turn, side, pl.ds(filled, count)]
        else:
            first, filled, count = LINES[m]
            src, dst = line_out.at[turn, pl.ds(first, count)], line_in.at[turn, pl.ds(filled, count)]
        return pltpu.make_async_remote_copy(
            src_ref=src, dst_ref=dst, send_sem=send_sem.at[turn, m], recv_sem=recv_sem.at[turn, m],
            device_id=(lat_of[STEPS[m][0]], lon_of[STEPS[m][1]]), device_id_type=MESH)

    def send_lines(turn):
        flat = jnp.concatenate([own[turn, r] for r in range(ROWS)], axis=1)
        picked = dot(flat, pack[...])
        picked = jnp.concatenate([picked, jnp.zeros((48, 128), F32)], axis=0)
        line_out[turn] = picked.T.astype(BF16)
        for m in range(4, 10):
            when_lat(STEPS[m][0], lambda m=m: copy_of(turn, m).start())

    def take_rows(turn, pad):
        for m in range(4):
            when_lat(-STEPS[m][0], lambda m=m: copy_of(turn, m).wait_recv())
        for r in range(3):
            pad[r] = edge_rows[turn, 0, r].astype(F32)[:WIDTH]
            pad[11 + r] = edge_rows[turn, 1, r].astype(F32)[:WIDTH]

    def take_lines(turn, slot, adjoint):
        for m in range(4, 10):
            when_lat(-STEPS[m][0], lambda m=m: copy_of(turn, m).wait_recv())
        lines = line_in[turn].astype(F32)
        for side in range(2):
            for k in range(3):
                base, at = 64 * side, 3 * side + k
                edges[slot, at, 0:3] = lines[base + 4 * k : base + 4 * k + 3]
                edges[slot, at, 3:11] = lines[base + 16 + 8 * k : base + 24 + 8 * k]
                edges[slot, at, 11:14] = lines[base + 48 + 4 * k : base + 51 + 4 * k]
        fixes = [jnp.zeros((8, SPAN), F32)] * 6
        for i in range(7):
            for side, x, k, j in MEETS:
                t = 48 - (7 * i + j) if adjoint else 7 * i + j
                fixes[3 * side + x] = fixes[3 * side + x] + tall[t : t + 1] * edges[slot, 3 * side + k, i : i + 8]
        total = jnp.concatenate(fixes, axis=0)
        coarse = total.astype(BF16).astype(F32)
        fix[...] = jnp.concatenate([coarse, total - coarse, jnp.zeros((32, SPAN), F32)], axis=0).T[:WIDTH].astype(BF16)

    def edge_depth(turn, slot, fresh):
        mine = line_out[turn].astype(F32)
        for i in range(7):
            for j in (0, 1, 2, 4, 5, 6):
                term = jnp.zeros((8, SPAN), F32)
                for side, x, k, at in MEETS:
                    if at == j:
                        base = (16 if side else 80) + 8 * x
                        term = term + mine[base : base + 8] * edges[slot, 3 * side + k, i : i + 8]
                term = jnp.sum(term, axis=0, keepdims=True)
                row = pl.ds(7 * i + j, 1)
                edge_terms[row] = term if fresh else edge_terms[row] + term

    def keep(turn, k, value, pad):
        rounded = value.astype(BF16)
        again = rounded.astype(F32)
        filled = jnp.concatenate([value, jnp.zeros((8, SPAN), F32)], axis=0).astype(BF16)
        for q in range(2):
            pad[3 + 2 * k + q] = again[:, COLS * q : COLS * (q + 1)]
            own[turn, 2 * k + q] = filled[:, COLS * q : COLS * (q + 1)]
        m = BAND_OF[k]
        if turn > 0:
            when_lat(STEPS[m][0], lambda: copy_of(turn, m).start())

    lane = lax.broadcasted_iota(jnp.int32, (1, 8, COLS), 2)

    def shifted(main, s):
        if s == 0:
            return main
        if s > 0:
            return pltpu.roll(jnp.where(lane < s, 0.0, main), COLS - s, 2)
        return pltpu.roll(jnp.where(lane >= COLS + s, 0.0, main), -s, 2)

    def tap(i, j, at, adjoint):
        return taps[48 - (7 * i + j) if adjoint else 7 * i + j, at, :][None]

    def depthwise(pad, target, adjoint, first_block=0, last_block=BLOCKS):
        def block(b, carry):
            at = pl.ds(pl.multiple_of(8 * b, 8), 8)
            main = pad[3:11, at, :]
            total = None
            for j in range(7):
                moved = shifted(main, j - 3)
                for i in (3, 0, 1, 2, 4, 5, 6):
                    low, high = max(0, 3 - i), min(8, 11 - i)
                    term = tap(i, j, at, adjoint) * moved[low + i - 3 : high + i - 3]
                    if total is None:
                        total = term
                        continue
                    pieces = [total[:low]] if low else []
                    pieces.append(total[low:high] + term)
                    pieces += [total[high:]] if high < 8 else []
                    total = jnp.concatenate(pieces, axis=0) if len(pieces) > 1 else pieces[0]
            target[:, at, :] = total
            return carry
        lax.fori_loop(first_block, last_block, block, 0)

    def depthwise_ends(pad, target, adjoint):
        def block(b, carry):
            at = pl.ds(pl.multiple_of(8 * b, 8), 8)
            top, bottom = pad[0:3, at, :], pad[11:14, at, :]
            high, low = [target[y, at, :][None] for y in range(3)], [target[5 + y, at, :][None] for y in range(3)]
            for j in range(7):
                above, below = shifted(top, j - 3), shifted(bottom, j - 3)
                for i in range(3):
                    weight, under = tap(i, j, at, adjoint), tap(6 - i, j, at, adjoint)
                    for y in range(3 - i):
                        high[y] = high[y] + weight * above[y + i : y + i + 1]
                        low[2 - y] = low[2 - y] + under * below[2 - y - i : 3 - y - i]
            for y in range(3):
                target[y, at, :] = high[y][0]
                target[5 + y, at, :] = low[y][0]
            return carry
        lax.fori_loop(0, BLOCKS, block, 0)

    def depth_terms(pad, fresh, first_block=0, last_block=BLOCKS):
        def block(b, carry):
            at = pl.ds(pl.multiple_of(8 * b, 8), 8)
            main, slope = pad[:, at, :], grad[:, at, :]
            for j in range(7):
                moved = shifted(main, j - 3)
                for i in range(7):
                    term = jnp.sum(slope * moved[i : i + ROWS], axis=0)
                    if fresh:
                        depth_acc[7 * i + j, at, :] = term
                    else:
                        depth_acc[7 * i + j, at, :] += term
            return carry
        lax.fori_loop(first_block, last_block, block, 0)

    def whole(k):
        return pair(conv, k) + dot(fix[...], spread[k])

    def over_chunks(body):
        for k in ORDER:
            body(k)

    def mask_of(k):
        both = jnp.concatenate([mask[pl.ds(2 * k, 1), :], mask[pl.ds(2 * k + 1, 1), :]], axis=1)
        return both.astype(F32)

    def levels_of(ref, k):
        return jnp.concatenate(
            [ref[pl.ds(2 * k + q, LEVELS, stride=ROWS), :] for q in range(2)], axis=1)

    tall[...] = jnp.zeros_like(tall)
    for i in range(7):
        tall[7 * i : 7 * i + 7, :WIDTH] = depth_in[i]
    tall[49:50, :WIDTH] = bias_in[...]
    tall[50:51, :WIDTH] = gain_in[...]
    params[...] = tall[...].T[:WIDTH]
    bias = params[:, 49:50]
    gain = params[:, 50:51]

    def encode(k, value, turn, pad):
        keep(turn, k, dot(encw[...], value.astype(BF16)) + bias, pad)

    over_chunks(lambda k: encode(k, levels_of(state, k), 0, pad_one))

    def ends(turn):
        @pl.when(jnp.logical_not(has_north))
        def _():
            edge_rows[turn, 0] = jnp.zeros_like(edge_rows[turn, 0])
            for part in (0, 64):
                line_in[turn, pl.ds(part, 16)] = jnp.zeros((16, SPAN), BF16)

        @pl.when(jnp.logical_not(has_south))
        def _():
            edge_rows[turn, 1] = jnp.zeros_like(edge_rows[turn, 1])
            for part in (48, 112):
                line_in[turn, pl.ds(part, 16)] = jnp.zeros((16, SPAN), BF16)

    peers = 24 + 3 * jnp.minimum(lat, 1) + 3 * jnp.minimum(lats - 1 - lat, 1)
    pl.semaphore_wait(barrier, peers)
    for m in range(4):
        when_lat(STEPS[m][0], lambda m=m: copy_of(0, m).start())
    send_lines(0)

    for turn in range(4):
        ends(turn)
    for t in range(49):
        taps[t] = jnp.broadcast_to(params[:, t : t + 1], (WIDTH, COLS))
    upw[...] = upt[...].astype(F32).T.astype(BF16)
    sums[...] = jnp.zeros_like(sums)
    edge_terms[...] = jnp.zeros_like(edge_terms)
    downt[...] = downw[...].astype(F32).T.astype(BF16)
    decw[...] = dect[...].astype(F32).T.astype(BF16)
    enct[...] = encw[...].astype(F32).T.astype(BF16)

    depthwise(pad_one, conv, False)
    take_rows(0, pad_one)
    depthwise_ends(pad_one, conv, False)
    take_lines(0, 0, False)

    def normalize(k, std, inv, normed):
        value = whole(k)
        centre = value - jnp.sum(value, axis=0, keepdims=True) * (1.0 / WIDTH)
        inverse = lax.rsqrt(jnp.sum(centre * centre, axis=0, keepdims=True) * (1.0 / WIDTH) + EPSILON)
        standard = centre * inverse
        std[2 * k], std[2 * k + 1] = rows_of(standard)
        inv[k] = jnp.broadcast_to(inverse, (8, SPAN))
        result = (standard * gain).astype(BF16)
        normed[k] = result
        return result

    def forward(k):
        ocean = mask_of(k)
        preact = dot(upw[...], normalize(k, std_one, inv_one, normed_one))
        value, slope = gelu_parts(preact)
        value = value.astype(BF16)
        act_one[k] = value
        slope_one[k] = slope.astype(BF16)
        features = jnp.concatenate([pad_one[3 + 2 * k], pad_one[4 + 2 * k]], axis=1)
        joined = (features + ocean * dot(downw[...], value)).astype(BF16)
        middle = levels_of(state, k) + ocean * dot(decw[...], joined)
        encode(k, middle, 1, pad_two)

    over_chunks(forward)
    send_lines(1)
    depthwise(pad_two, conv, False)
    take_rows(1, pad_two)
    depthwise_ends(pad_two, conv, False)
    take_lines(1, 1, False)

    def reverse(k, turn, upstream, normed, value, slope, std, inv):
        ocean = mask_of(k)
        grad_join = dot(dect[...], (ocean * upstream).astype(BF16))
        join[k] = grad_join
        grad_branch = (ocean * grad_join).astype(BF16)
        grad_pre = (dot(downt[...], grad_branch) * slope).astype(BF16)
        grad_norm = dot(upt[...], grad_pre)
        standard = pair(std, k)
        grad_hat = grad_norm * gain
        first = jnp.sum(grad_hat, axis=0, keepdims=True) * (1.0 / WIDTH)
        second = jnp.sum(grad_hat * standard, axis=0, keepdims=True) * (1.0 / WIDTH)
        result = inv[k][0:1] * (grad_hat - first - standard * second)
        grad[2 * k], grad[2 * k + 1] = rows_of(result)
        keep(turn, k, result, pad_g)
        for which, term in ((0, dot_nt(normed, grad_pre)), (1, dot_nt(grad_branch, value))):
            for part in range(3):
                sums[which, part, :WIDTH, :] += term[:, SPAN * part : SPAN * (part + 1)]
            sums[which, 3, :WIDTH, : HIDDEN - 3 * SPAN] += term[:, 3 * SPAN :]

    def late(k):
        normed = normalize(k, std_two, inv_two, normed_two)
        value, slope = gelu_parts(dot(upw[...], normed))
        reverse(k, 2, levels_of(cot, k), normed, value.astype(BF16), slope, std_two, inv_two)

    over_chunks(late)
    send_lines(2)
    depth_terms(pad_two, True)
    edge_depth(2, 1, True)
    depthwise(pad_g, conv, True)
    take_rows(2, pad_g)
    depthwise_ends(pad_g, conv, True)
    take_lines(2, 2, True)

    def early(k):
        grad_input = (join[k] + whole(k)).astype(BF16)
        upstream = levels_of(cot, k) + dot(enct[...], grad_input)
        grad_mid[k] = upstream
        reverse(k, 3, upstream, normed_one[k], act_one[k], slope_one[k].astype(F32), std_one, inv_one)

    over_chunks(early)
    send_lines(3)

    def remote(src, dst, slot, peer):
        return pltpu.make_async_remote_copy(
            src_ref=src, dst_ref=dst, send_sem=sum_send.at[slot], recv_sem=sum_recv.at[slot],
            device_id=peer, device_id_type=MESH)

    def line_at(d):
        return lax.rem(x_at + d, 4)

    mine = pl.ds(pl.multiple_of(16 * jnp.minimum(member, 12), 16), 16)
    halves = [remote(half_out.at[line_at(d)], half_in.at[line_at(d)], 75 + d, core_peer()) for d in range(4)]
    backs = [remote(gathered.at[core, line_at(d)], gathered.at[core, line_at(d)], 79 + d, core_peer()) for d in range(4)]
    quarters = [remote(quarter_out.at[line_at(d)], quarter_in.at[d - 1], d, line_peer(d)) for d in range(1, 4)]

    def slot_copy(d):
        other = jnp.minimum(member_at(d), 12)
        rows = pl.ds(pl.multiple_of(16 * other, 16), 16)
        return remote(slot_out.at[rows], slot_in.at[d - 1], 3 + d, plane_peer(d))

    def done_copy(d):
        return remote(slot_done, gathered.at[core, x_at, mine], 18 + d, plane_peer(d))

    def line_copy(d):
        return remote(gathered.at[core, x_at], gathered.at[core, x_at], 33 + d, line_peer(d))

    def depth_copy(d):
        return remote(depth_own.at[member_at(d)], depth_got.at[d - 1], 37 + d, plane_peer(d))

    def peer_copy(d):
        return remote(depth_mid, depth_peer.at[d - 1], 52 + d, chip_peer(d))

    def spread_copy(d):
        return remote(depth_all.at[member], depth_all.at[member], 59 + d, plane_peer(d))

    def owner(index):
        return lambda run: pl.when(index < 13)(run)

    for d in (1, 2, 3, 0):
        half_out[line_at(d)] = sums[1 - core, line_at(d)].astype(BF16)
        halves[d].start()
    depth_terms(pad_one, False, 0, 6)

    for d in (1, 2, 3):
        halves[d].wait_recv()
        quarter_out[line_at(d)] = (sums[core, line_at(d)] + half_in[line_at(d)].astype(F32)).astype(BF16)
        quarters[d - 1].start()
    halves[0].wait_recv()
    slot_sum[...] = sums[core, x_at] + half_in[x_at].astype(F32)
    depth_terms(pad_one, False, 6, BLOCKS)

    for copy in quarters:
        copy.wait_recv()
    slot_sum[...] = slot_sum[...] + (
        quarter_in[0].astype(F32) + quarter_in[1].astype(F32) + quarter_in[2].astype(F32))
    slot_out[...] = slot_sum[...].astype(BF16)
    for d in range(1, 16):
        owner(member_at(d))(lambda d=d: slot_copy(d).start())

    edge_depth(3, 0, False)
    column = lax.broadcasted_iota(jnp.int32, (WIDTH, COLS), 1)
    picked = jnp.zeros((WIDTH, COLS), F32)
    for t in range(49):
        picked = jnp.where(column == t, jnp.sum(depth_acc[t], axis=1, keepdims=True), picked)
    turned = jnp.concatenate([picked, jnp.zeros((56, COLS), F32)], axis=0).T[:64] + edge_terms[...]
    for piece in range(16):
        depth_own[piece] = turned[
            8 * (piece // 2) : 8 * (piece // 2) + 8, COLS * (piece % 2) : COLS * (piece % 2) + COLS]
    for d in range(1, 16):
        depth_copy(d).start()
    depthwise(pad_g, conv, True, 0, 10)

    @pl.when(member < 13)
    def _():
        total = slot_sum[mine, :]
        for d in range(1, 16):
            slot_copy(d).wait_recv()
            total = total + slot_in[d - 1].astype(F32)
        total = (total * scale).astype(BF16)
        slot_done[...] = total
        gathered[core, x_at, mine, :] = total
        for d in range(1, 16):
            done_copy(d).start()

    total = depth_own[member]
    for d in range(1, 16):
        depth_copy(d).wait_recv()
        total = total + depth_got[d - 1]
    depth_mid[...] = total
    for d in range(1, 8):
        peer_copy(d).start()
    depthwise(pad_g, conv, True, 10, BLOCKS)

    for d in range(1, 16):
        owner(member_at(16 - d))(lambda d=d: done_copy(d).wait_recv())
    for d in range(1, 4):
        line_copy(d).start()
    backs[0].start()
    total = depth_mid[...]
    for d in range(1, 8):
        peer_copy(d).wait_recv()
        total = total + depth_peer[d - 1]
    depth_all[member] = total * scale
    for d in range(1, 16):
        spread_copy(d).start()
    take_rows(3, pad_g)
    depthwise_ends(pad_g, conv, True)
    take_lines(3, 2, True)

    def last(k):
        grad_input = (join[k] + whole(k)).astype(BF16)
        result = grad_mid[k] + dot(enct[...], grad_input)
        for q in range(2):
            out[pl.ds(2 * k + q, LEVELS, stride=ROWS), :] = result[:, COLS * q : COLS * (q + 1)]

    over_chunks(last)
    for d in (1, 2, 3):
        line_copy(d).wait_recv()
        backs[4 - d].start()
    for d in range(1, 16):
        spread_copy(d).wait_recv()
    for piece in range(16):
        row, left = 8 * (piece // 2), COLS * (piece % 2)
        width = min(COLS, WIDTH - left)
        for t in range(row, min(row + 8, 49)):
            depth_out[t // 7, t % 7 : t % 7 + 1, left : left + width] = depth_all[piece, t - row : t - row + 1, :width]
    for copy in backs:
        copy.wait_recv()

    for copy in halves + quarters + backs:
        copy.wait_send()
    for d in range(1, 4):
        line_copy(d).wait_send()
    for d in range(1, 8):
        peer_copy(d).wait_send()
    for d in range(1, 16):
        owner(member_at(d))(lambda d=d: slot_copy(d).wait_send())
        owner(member)(lambda d=d: done_copy(d).wait_send())
        depth_copy(d).wait_send()
        spread_copy(d).wait_send()
    for turn in range(4):
        for m in range(10):
            when_lat(STEPS[m][0], lambda m=m: copy_of(turn, m).wait_send())


def main_call(scale, *operands):
    vmem = pl.BlockSpec(memory_space=pltpu.VMEM)
    padded = pltpu.VMEM((14, WIDTH, COLS), F32)
    plane = pltpu.VMEM((ROWS, WIDTH, COLS), F32)
    tile = (8, COLS)
    return pl.pallas_call(
        functools.partial(main_kernel, scale),
        out_shape=[
            jax.ShapeDtypeStruct((LEVELS * ROWS, COLS), F32),
            jax.ShapeDtypeStruct((2, 4, 208, SPAN), BF16),
            jax.ShapeDtypeStruct((7, 7, WIDTH), F32),
        ],
        in_specs=[vmem] * len(operands),
        out_specs=[vmem] * 3,
        scratch_shapes=[
            pltpu.VMEM((49, WIDTH, COLS), F32),
            padded, padded, padded,
            plane, plane, plane, plane,
            pltpu.VMEM((CHUNKS, 8, SPAN), F32),
            pltpu.VMEM((CHUNKS, 8, SPAN), F32),
            pltpu.VMEM((CHUNKS, HIDDEN, SPAN), BF16),
            pltpu.VMEM((CHUNKS, HIDDEN, SPAN), BF16),
            pltpu.VMEM((CHUNKS, WIDTH, SPAN), BF16),
            pltpu.VMEM((CHUNKS, WIDTH, SPAN), BF16),
            pltpu.VMEM((CHUNKS, WIDTH, SPAN), F32),
            pltpu.VMEM((CHUNKS, LEVELS, SPAN), F32),
            pltpu.VMEM((49, WIDTH, COLS), F32),
            pltpu.VMEM((HIDDEN, WIDTH), BF16),
            pltpu.VMEM((HIDDEN, WIDTH), BF16),
            pltpu.VMEM((LEVELS, WIDTH), BF16),
            pltpu.VMEM((LEVELS, WIDTH), BF16),
            pltpu.VMEM((4, ROWS, 208, COLS), BF16),
            pltpu.VMEM((4, 2, 3, 208, COLS), BF16),
            pltpu.VMEM((4, 128, SPAN), BF16),
            pltpu.VMEM((4, 128, SPAN), BF16),
            pltpu.SemaphoreType.DMA((4, 10)),
            pltpu.SemaphoreType.DMA((4, 10)),
            pltpu.VMEM((128, SPAN), F32),
            pltpu.VMEM((WIDTH, COLS), F32),
            pltpu.VMEM((2, 4, 208, SPAN), F32),
            pltpu.VMEM((4, 208, SPAN), BF16),
            pltpu.VMEM((4, 208, SPAN), BF16),
            pltpu.VMEM((4, 208, SPAN), BF16),
            pltpu.VMEM((3, 208, SPAN), BF16),
            pltpu.VMEM((208, SPAN), F32),
            pltpu.VMEM((208, SPAN), BF16),
            pltpu.VMEM((15, 16, SPAN), BF16),
            pltpu.VMEM((16, SPAN), BF16),
            pltpu.VMEM((16,) + tile, F32),
            pltpu.VMEM((15,) + tile, F32),
            pltpu.VMEM(tile, F32),
            pltpu.VMEM((7,) + tile, F32),
            pltpu.VMEM((16,) + tile, F32),
            pltpu.SemaphoreType.DMA((83,)),
            pltpu.SemaphoreType.DMA((83,)),
            pltpu.VMEM((3, 6, 16, SPAN), F32),
            pltpu.VMEM((WIDTH, COLS), BF16),
            pltpu.VMEM((64, SPAN), F32),
        ],
        compiler_params=pltpu.CompilerParams(
            collective_id=0, has_side_effects=True, vmem_limit_bytes=58 * 1024 * 1024),
    )(*operands)


def result_kernel(state, gathered, depth, state_out, up_out, down_out, depth_out):
    state_out[...] = state[...]
    depth_out[...] = depth[...]
    for which, target in ((0, up_out), (1, down_out)):
        for part in range(4):
            left = SPAN * part
            width = min(SPAN, HIDDEN - left)
            target[:, left : left + width] = gathered[which, part].astype(F32)[:WIDTH, :width]


def result_call(*operands):
    vmem = pl.BlockSpec(memory_space=pltpu.VMEM)
    return pl.pallas_call(
        result_kernel,
        out_shape=[
            jax.ShapeDtypeStruct((LEVELS * ROWS, COLS), F32),
            jax.ShapeDtypeStruct((WIDTH, HIDDEN), F32),
            jax.ShapeDtypeStruct((WIDTH, HIDDEN), F32),
            jax.ShapeDtypeStruct((7, 7, WIDTH), F32),
        ],
        in_specs=[vmem] * 3,
        out_specs=[vmem] * 4,
    )(*operands)


def per_device(
    ocean_state, ocean_mask, cotangent, encoder_weight, encoder_bias, depth_weight,
    norm_gain, up_weight, down_weight, decoder_weight,
):
    cells = ROWS * lax.axis_size("lat") * COLS * lax.axis_size("lon")
    pack, spread = edge_tables()
    parts = main_call(
        1.0 / math.sqrt(cells),
        ocean_state.reshape(LEVELS * ROWS, COLS), ocean_mask, cotangent.reshape(LEVELS * ROWS, COLS),
        encoder_weight, encoder_bias[None, :], jnp.transpose(depth_weight, (1, 2, 0)), norm_gain[None, :],
        up_weight.T, down_weight, decoder_weight.T, jnp.asarray(pack), jnp.asarray(spread))
    state_grad, up_sum, down_sum, depth_sum = result_call(*parts)
    return (
        state_grad.reshape(ocean_state.shape),
        up_sum.T,
        down_sum,
        jnp.transpose(depth_sum, (2, 0, 1)),
    )


def solution(mesh):
    return jax.shard_map(
        per_device,
        mesh=mesh,
        in_specs=(
            P(None, "lat", "lon"), P("lat", "lon"), P(None, "lat", "lon"),
            P(), P(), P(), P(), P(), P(), P(),
        ),
        out_specs=(P(None, "lat", "lon"), P(), P(), P()),
        check_vma=False,
    )
```

```python
import functools
import math

import jax
import jax.numpy as jnp
import numpy as np
from jax import lax
from jax.experimental import pallas as pl
from jax.experimental.pallas import tpu as pltpu
from jax.sharding import PartitionSpec as P

EPSILON = 1e-06
GELU_SCALE = 0.7978845608028654
GELU_CUBE = 0.044715
MESH = pl.DeviceIdType.MESH
F32 = jnp.float32
BF16 = jnp.bfloat16
LEVELS = 100
WIDTH = 200
HIDDEN = 800
ROWS = 8
COLS = 128
CHUNKS = 4
SPAN = 256
FULL = 208
BLOCKS = FULL // 16

STEPS = ((-1, 0), (1, 0), (1, 0), (-1, 0), (0, 1), (0, -1), (1, 1), (1, -1), (-1, 1), (-1, -1))
BANDS = ((0, 1, 0, 2), (6, 0, 1, 2), (5, 0, 0, 1), (2, 1, 2, 1))
LINES = {4: (16, 16, 32), 5: (80, 80, 32), 6: (48, 0, 16), 7: (112, 64, 16), 8: (0, 48, 16), 9: (64, 112, 16)}
ORDER = (0, 3, 2, 1)
BAND_OF = {0: 0, 3: 1, 2: 2, 1: 3}
MEETS = tuple((0, x, k, k - x) for x in range(3) for k in range(x, 3)) + tuple(
    (1, x, k, 6 + k - x) for x in range(3) for k in range(x + 1))


def edge_tables():
    pack = np.zeros((ROWS * COLS, 128), np.float32)
    spread = np.zeros((CHUNKS, 128, SPAN), np.float32)
    for side in range(2):
        for k in range(3):
            column = k if side else 125 + k
            for first, step, sent, rows in ((0, 4, 0, 3), (16, 8, 0, 8), (48, 4, 5, 3)):
                for r in range(rows):
                    pack[COLS * (sent + r) + column, 64 * side + first + step * k + r] = 1.0
            for y in range(ROWS):
                column = 125 + k if side else k
                for part in (0, 48):
                    spread[y // 2, part + 24 * side + 8 * k + y, COLS * (y % 2) + column] = 1.0
    return pack.astype(jnp.bfloat16), spread.astype(jnp.bfloat16)


def dot(a, b):
    return jnp.dot(a, b, preferred_element_type=F32)


def dot_nt(a, b):
    return lax.dot_general(a, b, (((1,), (1,)), ((), ())), preferred_element_type=F32)


def gelu_parts(p):
    square = p * p
    half = 0.5 * jnp.tanh(p * (GELU_SCALE + (GELU_SCALE * GELU_CUBE) * square)) + 0.5
    value = p * half
    slope = half + value * (1.0 - half) * (2.0 * GELU_SCALE + (6.0 * GELU_SCALE * GELU_CUBE) * square)
    return value, slope


def rows_of(value):
    return value[:, :COLS], value[:, COLS:]


def pair(ref, k):
    return jnp.concatenate([ref[2 * k], ref[2 * k + 1]], axis=1)


INPUTS = 12
FIRST = (0, 1, 3, 4, 5, 6)


def staged_kernel(scale, *refs):
    raw, rest, buffers, sems = refs[:INPUTS], refs[INPUTS : -INPUTS - 1], refs[-INPUTS - 1 : -1], refs[-1]
    copies = [pltpu.make_async_copy(raw[n], buffers[n], sems.at[n]) for n in range(INPUTS)]

    def start():
        for n in FIRST + tuple(n for n in range(INPUTS) if n not in FIRST):
            copies[n].start()

    def arrive(first):
        for n in range(INPUTS):
            if (n in FIRST) == first:
                copies[n].wait()

    main_kernel(scale, start, arrive, *buffers, *rest)


def main_kernel(
    scale, start, arrive, state, mask, cot, encw, bias_in, depth_in, gain_in, upt, downw, dect, pack, spread,
    out, gathered, depth_out,
    taps, conv, std_one, std_two, inv_one, inv_two,
    act_one, slope_one, normed_one, normed_two, join, grad_mid, depth_acc,
    upw, downt, decw, enct, own, edge_rows, line_out, line_in, send_sem, recv_sem,
    tall, params, sums, half_out, half_in, quarter_out, quarter_in, slot_sum, slot_out, slot_in, slot_done,
    depth_own, depth_got, depth_mid, depth_peer, depth_all, sum_send, sum_recv,
    edges, fix, edge_terms,
):
    start()
    lat, lon = lax.axis_index("lat"), lax.axis_index("lon")
    lats, lons = lax.axis_size("lat"), lax.axis_size("lon")
    has_north, has_south = lat > 0, lat < lats - 1
    north, south = lat - 1, lat + 1
    east, west = lax.rem(lon + 1, lons), lax.rem(lon + lons - 1, lons)
    x_at, core = lat // 4, lax.rem(lat, 2)
    member = lon // 2 * 4 + lax.rem(lon, 2) * 2 + lax.rem(lat // 2, 2)

    def core_peer():
        return (lat + 1 - 2 * core, lon)

    def line_peer(d):
        return (lax.rem(x_at + d, 4) * 4 + lax.rem(lat, 4), lon)

    def chip_peer(d):
        flip, step = d // 4, d % 4
        side = 1 - core if flip else core
        return (lax.rem(x_at + step, 4) * 4 + lax.rem(lat // 2, 2) * 2 + side, lon)

    def member_at(d):
        return lax.rem(member + d, 16)

    def plane_peer(d):
        other = member_at(d)
        z_at, y_at = other // 4, lax.rem(other, 4)
        return (x_at * 4 + lax.rem(y_at, 2) * 2 + core, z_at * 2 + y_at // 2)

    lat_of = {0: lat, 1: south, -1: north}
    lon_of = {0: lon, 1: east, -1: west}

    def when_lat(step, run):
        if step == 0:
            run()
        elif step > 0:
            pl.when(has_south)(run)
        else:
            pl.when(has_north)(run)

    barrier = pltpu.get_barrier_semaphore()
    for step_lat, step_lon in STEPS[2:]:
        when_lat(step_lat, lambda a=step_lat, b=step_lon: pl.semaphore_signal(
            barrier, inc=1, device_id=(lat_of[a], lon_of[b]), device_id_type=MESH))

    for peer in [chip_peer(d) for d in range(1, 8)] + [plane_peer(d) for d in range(1, 16)]:
        pl.semaphore_signal(barrier, inc=1, device_id=peer, device_id_type=MESH)

    def copy_of(turn, m):
        if m < 4:
            first, side, filled, count = BANDS[m]
            src = own.at[turn, pl.ds(first, count)]
            dst = edge_rows.at[turn, side, pl.ds(filled, count)]
        else:
            first, filled, count = LINES[m]
            src, dst = line_out.at[turn, pl.ds(first, count)], line_in.at[turn, pl.ds(filled, count)]
        return pltpu.make_async_remote_copy(
            src_ref=src, dst_ref=dst, send_sem=send_sem.at[turn, m], recv_sem=recv_sem.at[turn, m],
            device_id=(lat_of[STEPS[m][0]], lon_of[STEPS[m][1]]), device_id_type=MESH)

    def send_lines(turn):
        flat = jnp.concatenate([own[turn, r] for r in range(ROWS)], axis=1)
        picked = dot(flat, pack[...])
        picked = jnp.concatenate([picked, jnp.zeros((48, 128), F32)], axis=0)
        line_out[turn] = picked.T.astype(BF16)
        for m in range(4, 10):
            when_lat(STEPS[m][0], lambda m=m: copy_of(turn, m).start())

    def take_rows(turn):
        for m in range(4):
            when_lat(-STEPS[m][0], lambda m=m: copy_of(turn, m).wait_recv())

    def take_lines(turn, slot, adjoint):
        for m in range(4, 10):
            when_lat(-STEPS[m][0], lambda m=m: copy_of(turn, m).wait_recv())
        lines = line_in[turn].astype(F32)
        for side in range(2):
            for k in range(3):
                base, at = 64 * side, 3 * side + k
                edges[slot, at, 0:3] = lines[base + 4 * k : base + 4 * k + 3]
                edges[slot, at, 3:11] = lines[base + 16 + 8 * k : base + 24 + 8 * k]
                edges[slot, at, 11:14] = lines[base + 48 + 4 * k : base + 51 + 4 * k]
        fixes = [jnp.zeros((8, SPAN), F32)] * 6
        for i in range(7):
            for side, x, k, j in MEETS:
                t = 48 - (7 * i + j) if adjoint else 7 * i + j
                fixes[3 * side + x] = fixes[3 * side + x] + tall[t : t + 1] * edges[slot, 3 * side + k, i : i + 8]
        total = jnp.concatenate(fixes, axis=0)
        coarse = total.astype(BF16).astype(F32)
        fix[...] = jnp.concatenate([coarse, total - coarse, jnp.zeros((32, SPAN), F32)], axis=0).T[:WIDTH].astype(BF16)

    def edge_depth(turn, slot, fresh):
        mine = line_out[turn].astype(F32)
        for i in range(7):
            for j in (0, 1, 2, 4, 5, 6):
                term = jnp.zeros((8, SPAN), F32)
                for side, x, k, at in MEETS:
                    if at == j:
                        base = (16 if side else 80) + 8 * x
                        term = term + mine[base : base + 8] * edges[slot, 3 * side + k, i : i + 8]
                term = jnp.sum(term, axis=0, keepdims=True)
                row = pl.ds(7 * i + j, 1)
                edge_terms[row] = term if fresh else edge_terms[row] + term

    def keep(turn, k, value):
        filled = jnp.concatenate([value, jnp.zeros((8, SPAN), F32)], axis=0).astype(BF16)
        own[turn, 2 * k], own[turn, 2 * k + 1] = rows_of(filled)
        m = BAND_OF[k]
        if turn > 0:
            when_lat(STEPS[m][0], lambda: copy_of(turn, m).start())

    lane = lax.broadcasted_iota(jnp.int32, (1, 16, COLS), 2)
    nothing = jnp.zeros((), BF16)

    def shifted(main, s):
        if s == 0:
            return main
        if s > 0:
            return pltpu.roll(jnp.where(lane < s, nothing, main), COLS - s, 2)
        return pltpu.roll(jnp.where(lane >= COLS + s, nothing, main), -s, 2)

    def tap(i, j, at, adjoint):
        return taps[48 - (7 * i + j) if adjoint else 7 * i + j, at, :][None]

    def over_blocks(body, first_block, last_block):
        def block(b, carry):
            body(pl.ds(pl.multiple_of(16 * b, 16), 16))
            return carry
        lax.fori_loop(first_block, last_block, block, 0, unroll=3 if last_block - first_block > 4 else 1)

    def depthwise(turn, adjoint, first_block=0, last_block=BLOCKS):
        def block(at):
            main = own[turn, :, at, :]
            total = None
            for j in range(7):
                moved = shifted(main, j - 3)
                part = None
                for i in (3, 0, 1, 2, 4, 5, 6):
                    low, high = max(0, 3 - i), min(8, 11 - i)
                    term = tap(i, j, at, adjoint) * moved[low + i - 3 : high + i - 3]
                    if part is None:
                        part = term
                        continue
                    pieces = [part[:low]] if low else []
                    pieces.append(part[low:high] + term)
                    pieces += [part[high:]] if high < 8 else []
                    part = jnp.concatenate(pieces, axis=0)
                part = part.astype(F32)
                total = part if total is None else total + part
            conv[:, at, :] = total
        over_blocks(block, first_block, last_block)

    def depthwise_ends(turn, adjoint):
        def block(at):
            top, bottom = edge_rows[turn, 0, :, at, :], edge_rows[turn, 1, :, at, :]
            high, low = conv[0:3, at, :], conv[5:8, at, :]
            for j in range(7):
                above, below = shifted(top, j - 3), shifted(bottom, j - 3)
                over, under = [None] * 3, [None] * 3
                for i in range(3):
                    weight, mirror = tap(i, j, at, adjoint), tap(6 - i, j, at, adjoint)
                    for y in range(3 - i):
                        term = weight * above[y + i : y + i + 1]
                        over[y] = term if over[y] is None else over[y] + term
                        term = mirror * below[2 - y - i : 3 - y - i]
                        under[2 - y] = term if under[2 - y] is None else under[2 - y] + term
                high = high + jnp.concatenate(over, axis=0).astype(F32)
                low = low + jnp.concatenate(under, axis=0).astype(F32)
            conv[0:3, at, :] = high
            conv[5:8, at, :] = low
        over_blocks(block, 0, BLOCKS)

    def depth_terms(turn, upper, fresh, first_block=0, last_block=BLOCKS):
        def block(at):
            main = jnp.concatenate(
                [edge_rows[turn, 0, :, at, :], own[turn, :, at, :], edge_rows[turn, 1, :, at, :]], axis=0)
            slope = own[upper, :, at, :]
            for j in range(7):
                moved = shifted(main, j - 3)
                for i in range(7):
                    product = slope * moved[i : i + ROWS]
                    term = product[0]
                    for y in range(1, ROWS):
                        term = term + product[y]
                    term = term.astype(F32)
                    if fresh:
                        depth_acc[7 * i + j, at, :] = term
                    else:
                        depth_acc[7 * i + j, at, :] += term
        over_blocks(block, first_block, last_block)

    def whole(k):
        return pair(conv, k)[:WIDTH] + dot(fix[...], spread[k])

    def over_chunks(body):
        for k in ORDER:
            body(k)

    def mask_of(k):
        both = jnp.concatenate([mask[pl.ds(2 * k, 1), :], mask[pl.ds(2 * k + 1, 1), :]], axis=1)
        return both.astype(F32)

    def levels_of(ref, k):
        return jnp.concatenate(
            [ref[pl.ds(2 * k + q, LEVELS, stride=ROWS), :] for q in range(2)], axis=1)

    arrive(True)
    tall[...] = jnp.zeros_like(tall)
    for i in range(7):
        tall[7 * i : 7 * i + 7, :WIDTH] = depth_in[i]
    tall[49:50, :WIDTH] = bias_in[...]
    tall[50:51, :WIDTH] = gain_in[...]
    params[...] = tall[...].T[:FULL]
    bias = params[:WIDTH, 49:50]
    gain = params[:WIDTH, 50:51]

    def encode(k, value, turn):
        keep(turn, k, dot(encw[...], value.astype(BF16)) + bias)

    over_chunks(lambda k: encode(k, levels_of(state, k), 0))

    def ends(turn):
        @pl.when(jnp.logical_not(has_north))
        def _():
            edge_rows[turn, 0] = jnp.zeros_like(edge_rows[turn, 0])
            for part in (0, 64):
                line_in[turn, pl.ds(part, 16)] = jnp.zeros((16, SPAN), BF16)

        @pl.when(jnp.logical_not(has_south))
        def _():
            edge_rows[turn, 1] = jnp.zeros_like(edge_rows[turn, 1])
            for part in (48, 112):
                line_in[turn, pl.ds(part, 16)] = jnp.zeros((16, SPAN), BF16)

    arrive(False)
    peers = 24 + 3 * jnp.minimum(lat, 1) + 3 * jnp.minimum(lats - 1 - lat, 1)
    pl.semaphore_wait(barrier, peers)
    for m in range(4):
        when_lat(STEPS[m][0], lambda m=m: copy_of(0, m).start())
    send_lines(0)

    for turn in range(4):
        ends(turn)
    for t in range(49):
        taps[t] = jnp.broadcast_to(params[:, t : t + 1], (FULL, COLS)).astype(BF16)
    upw[...] = upt[...].astype(F32).T.astype(BF16)
    sums[...] = jnp.zeros_like(sums)
    edge_terms[...] = jnp.zeros_like(edge_terms)
    downt[...] = downw[...].astype(F32).T.astype(BF16)
    decw[...] = dect[...].astype(F32).T.astype(BF16)
    enct[...] = encw[...].astype(F32).T.astype(BF16)

    depthwise(0, False)
    take_rows(0)
    depthwise_ends(0, False)
    take_lines(0, 0, False)

    def normalize(k, std, inv, normed):
        value = whole(k)
        centre = value - jnp.sum(value, axis=0, keepdims=True) * (1.0 / WIDTH)
        inverse = lax.rsqrt(jnp.sum(centre * centre, axis=0, keepdims=True) * (1.0 / WIDTH) + EPSILON)
        standard = centre * inverse
        std[2 * k], std[2 * k + 1] = rows_of(standard)
        inv[k] = jnp.broadcast_to(inverse, (8, SPAN))
        result = (standard * gain).astype(BF16)
        normed[k] = result
        return result

    def forward(k):
        ocean = mask_of(k)
        preact = dot(upw[...], normalize(k, std_one, inv_one, normed_one))
        value, slope = gelu_parts(preact)
        value = value.astype(BF16)
        act_one[k] = value
        slope_one[k] = slope.astype(BF16)
        features = pair(own.at[0], k).astype(F32)[:WIDTH]
        joined = (features + ocean * dot(downw[...], value)).astype(BF16)
        middle = levels_of(state, k) + ocean * dot(decw[...], joined)
        encode(k, middle, 1)

    over_chunks(forward)
    send_lines(1)
    depthwise(1, False)
    take_rows(1)
    depthwise_ends(1, False)
    take_lines(1, 1, False)

    def reverse(k, turn, upstream, normed, value, slope, std, inv):
        ocean = mask_of(k)
        grad_join = dot(dect[...], (ocean * upstream).astype(BF16))
        join[k] = grad_join
        grad_branch = (ocean * grad_join).astype(BF16)
        grad_pre = (dot(downt[...], grad_branch) * slope).astype(BF16)
        grad_norm = dot(upt[...], grad_pre)
        standard = pair(std, k)
        grad_hat = grad_norm * gain
        first = jnp.sum(grad_hat, axis=0, keepdims=True) * (1.0 / WIDTH)
        second = jnp.sum(grad_hat * standard, axis=0, keepdims=True) * (1.0 / WIDTH)
        result = inv[k][0:1] * (grad_hat - first - standard * second)
        keep(turn, k, result)
        for which, term in ((0, dot_nt(normed, grad_pre)), (1, dot_nt(grad_branch, value))):
            for part in range(3):
                sums[which, part, :WIDTH, :] += term[:, SPAN * part : SPAN * (part + 1)]
            sums[which, 3, :WIDTH, : HIDDEN - 3 * SPAN] += term[:, 3 * SPAN :]

    def late(k):
        normed = normalize(k, std_two, inv_two, normed_two)
        value, slope = gelu_parts(dot(upw[...], normed))
        reverse(k, 2, levels_of(cot, k), normed, value.astype(BF16), slope, std_two, inv_two)

    over_chunks(late)
    send_lines(2)
    depth_terms(1, 2, True)
    edge_depth(2, 1, True)
    depthwise(2, True)
    take_rows(2)
    depthwise_ends(2, True)
    take_lines(2, 2, True)

    def early(k):
        grad_input = (join[k] + whole(k)).astype(BF16)
        upstream = levels_of(cot, k) + dot(enct[...], grad_input)
        grad_mid[k] = upstream
        reverse(k, 3, upstream, normed_one[k], act_one[k], slope_one[k].astype(F32), std_one, inv_one)

    over_chunks(early)
    send_lines(3)

    def remote(src, dst, slot, peer):
        return pltpu.make_async_remote_copy(
            src_ref=src, dst_ref=dst, send_sem=sum_send.at[slot], recv_sem=sum_recv.at[slot],
            device_id=peer, device_id_type=MESH)

    def line_at(d):
        return lax.rem(x_at + d, 4)

    mine = pl.ds(pl.multiple_of(16 * jnp.minimum(member, 12), 16), 16)
    halves = [remote(half_out.at[line_at(d)], half_in.at[line_at(d)], 75 + d, core_peer()) for d in range(4)]
    backs = [remote(gathered.at[core, line_at(d)], gathered.at[core, line_at(d)], 79 + d, core_peer()) for d in range(4)]
    quarters = [remote(quarter_out.at[line_at(d)], quarter_in.at[d - 1], d, line_peer(d)) for d in range(1, 4)]

    def slot_copy(d):
        other = jnp.minimum(member_at(d), 12)
        rows = pl.ds(pl.multiple_of(16 * other, 16), 16)
        return remote(slot_out.at[rows], slot_in.at[d - 1], 3 + d, plane_peer(d))

    def done_copy(d):
        return remote(slot_done, gathered.at[core, x_at, mine], 18 + d, plane_peer(d))

    def line_copy(d):
        return remote(gathered.at[core, x_at], gathered.at[core, x_at], 33 + d, line_peer(d))

    def depth_copy(d):
        return remote(depth_own.at[member_at(d)], depth_got.at[d - 1], 37 + d, plane_peer(d))

    def peer_copy(d):
        return remote(depth_mid, depth_peer.at[d - 1], 52 + d, chip_peer(d))

    def spread_copy(d):
        return remote(depth_all.at[member], depth_all.at[member], 59 + d, plane_peer(d))

    def owner(index):
        return lambda run: pl.when(index < 13)(run)

    for d in (1, 2, 3, 0):
        half_out[line_at(d)] = sums[1 - core, line_at(d)].astype(BF16)
        halves[d].start()
    depth_terms(0, 3, False, 0, 3)

    for d in (1, 2, 3):
        halves[d].wait_recv()
        quarter_out[line_at(d)] = (sums[core, line_at(d)] + half_in[line_at(d)].astype(F32)).astype(BF16)
        quarters[d - 1].start()
    halves[0].wait_recv()
    slot_sum[...] = sums[core, x_at] + half_in[x_at].astype(F32)
    depth_terms(0, 3, False, 3, BLOCKS)

    for copy in quarters:
        copy.wait_recv()
    slot_sum[...] = slot_sum[...] + (
        quarter_in[0].astype(F32) + quarter_in[1].astype(F32) + quarter_in[2].astype(F32))
    slot_out[...] = slot_sum[...].astype(BF16)
    for d in range(1, 16):
        owner(member_at(d))(lambda d=d: slot_copy(d).start())

    edge_depth(3, 0, False)
    column = lax.broadcasted_iota(jnp.int32, (FULL, COLS), 1)
    picked = jnp.zeros((FULL, COLS), F32)
    for t in range(49):
        picked = jnp.where(column == t, jnp.sum(depth_acc[t], axis=1, keepdims=True), picked)
    turned = jnp.concatenate([picked, jnp.zeros((48, COLS), F32)], axis=0).T[:64] + edge_terms[...]
    for piece in range(16):
        depth_own[piece] = turned[
            8 * (piece // 2) : 8 * (piece // 2) + 8, COLS * (piece % 2) : COLS * (piece % 2) + COLS]
    for d in range(1, 16):
        depth_copy(d).start()
    depthwise(3, True, 0, 5)

    @pl.when(member < 13)
    def _():
        total = slot_sum[mine, :]
        for d in range(1, 16):
            slot_copy(d).wait_recv()
            total = total + slot_in[d - 1].astype(F32)
        total = (total * scale).astype(BF16)
        slot_done[...] = total
        gathered[core, x_at, mine, :] = total
        for d in range(1, 16):
            done_copy(d).start()

    total = depth_own[member]
    for d in range(1, 16):
        depth_copy(d).wait_recv()
        total = total + depth_got[d - 1]
    depth_mid[...] = total
    for d in range(1, 8):
        peer_copy(d).start()
    depthwise(3, True, 5, BLOCKS)

    for d in range(1, 16):
        owner(member_at(16 - d))(lambda d=d: done_copy(d).wait_recv())
    for d in range(1, 4):
        line_copy(d).start()
    backs[0].start()
    total = depth_mid[...]
    for d in range(1, 8):
        peer_copy(d).wait_recv()
        total = total + depth_peer[d - 1]
    depth_all[member] = total * scale
    for d in range(1, 16):
        spread_copy(d).start()
    take_rows(3)
    depthwise_ends(3, True)
    take_lines(3, 2, True)

    def last(k):
        grad_input = (join[k] + whole(k)).astype(BF16)
        result = grad_mid[k] + dot(enct[...], grad_input)
        for q in range(2):
            out[pl.ds(2 * k + q, LEVELS, stride=ROWS), :] = result[:, COLS * q : COLS * (q + 1)]

    over_chunks(last)
    for d in (1, 2, 3):
        line_copy(d).wait_recv()
        backs[4 - d].start()
    for d in range(1, 16):
        spread_copy(d).wait_recv()
    for piece in range(16):
        row, left = 8 * (piece // 2), COLS * (piece % 2)
        width = min(COLS, WIDTH - left)
        for t in range(row, min(row + 8, 49)):
            depth_out[t // 7, t % 7 : t % 7 + 1, left : left + width] = depth_all[piece, t - row : t - row + 1, :width]
    for copy in backs:
        copy.wait_recv()

    for copy in halves + quarters + backs:
        copy.wait_send()
    for d in range(1, 4):
        line_copy(d).wait_send()
    for d in range(1, 8):
        peer_copy(d).wait_send()
    for d in range(1, 16):
        owner(member_at(d))(lambda d=d: slot_copy(d).wait_send())
        owner(member)(lambda d=d: done_copy(d).wait_send())
        depth_copy(d).wait_send()
        spread_copy(d).wait_send()
    for turn in range(4):
        for m in range(10):
            when_lat(STEPS[m][0], lambda m=m: copy_of(turn, m).wait_send())


def main_call(scale, *operands):
    vmem = pl.BlockSpec(memory_space=pltpu.VMEM)
    plane = pltpu.VMEM((ROWS, WIDTH, COLS), F32)
    tile = (8, COLS)
    return pl.pallas_call(
        functools.partial(staged_kernel, scale),
        out_shape=[
            jax.ShapeDtypeStruct((LEVELS * ROWS, COLS), F32),
            jax.ShapeDtypeStruct((2, 4, 208, SPAN), BF16),
            jax.ShapeDtypeStruct((7, 7, WIDTH), F32),
        ],
        in_specs=[pl.BlockSpec(memory_space=pl.ANY)] * len(operands),
        out_specs=[vmem] * 3,
        scratch_shapes=[
            pltpu.VMEM((49, FULL, COLS), BF16),
            pltpu.VMEM((ROWS, FULL, COLS), F32),
            plane, plane,
            pltpu.VMEM((CHUNKS, 8, SPAN), F32),
            pltpu.VMEM((CHUNKS, 8, SPAN), F32),
            pltpu.VMEM((CHUNKS, HIDDEN, SPAN), BF16),
            pltpu.VMEM((CHUNKS, HIDDEN, SPAN), BF16),
            pltpu.VMEM((CHUNKS, WIDTH, SPAN), BF16),
            pltpu.VMEM((CHUNKS, WIDTH, SPAN), BF16),
            pltpu.VMEM((CHUNKS, WIDTH, SPAN), F32),
            pltpu.VMEM((CHUNKS, LEVELS, SPAN), F32),
            pltpu.VMEM((49, FULL, COLS), F32),
            pltpu.VMEM((HIDDEN, WIDTH), BF16),
            pltpu.VMEM((HIDDEN, WIDTH), BF16),
            pltpu.VMEM((LEVELS, WIDTH), BF16),
            pltpu.VMEM((LEVELS, WIDTH), BF16),
            pltpu.VMEM((4, ROWS, 208, COLS), BF16),
            pltpu.VMEM((4, 2, 3, 208, COLS), BF16),
            pltpu.VMEM((4, 128, SPAN), BF16),
            pltpu.VMEM((4, 128, SPAN), BF16),
            pltpu.SemaphoreType.DMA((4, 10)),
            pltpu.SemaphoreType.DMA((4, 10)),
            pltpu.VMEM((128, SPAN), F32),
            pltpu.VMEM((FULL, COLS), F32),
            pltpu.VMEM((2, 4, 208, SPAN), F32),
            pltpu.VMEM((4, 208, SPAN), BF16),
            pltpu.VMEM((4, 208, SPAN), BF16),
            pltpu.VMEM((4, 208, SPAN), BF16),
            pltpu.VMEM((3, 208, SPAN), BF16),
            pltpu.VMEM((208, SPAN), F32),
            pltpu.VMEM((208, SPAN), BF16),
            pltpu.VMEM((15, 16, SPAN), BF16),
            pltpu.VMEM((16, SPAN), BF16),
            pltpu.VMEM((16,) + tile, F32),
            pltpu.VMEM((15,) + tile, F32),
            pltpu.VMEM(tile, F32),
            pltpu.VMEM((7,) + tile, F32),
            pltpu.VMEM((16,) + tile, F32),
            pltpu.SemaphoreType.DMA((83,)),
            pltpu.SemaphoreType.DMA((83,)),
            pltpu.VMEM((3, 6, 16, SPAN), F32),
            pltpu.VMEM((WIDTH, COLS), BF16),
            pltpu.VMEM((64, SPAN), F32),
            *[pltpu.VMEM(value.shape, value.dtype) for value in operands],
            pltpu.SemaphoreType.DMA((INPUTS,)),
        ],
        compiler_params=pltpu.CompilerParams(
            collective_id=0, has_side_effects=True, vmem_limit_bytes=58 * 1024 * 1024),
    )(*operands)


def result_kernel(state, gathered, depth, state_out, up_out, down_out, depth_out):
    state_out[...] = state[...]
    depth_out[...] = depth[...]
    for which, target in ((0, up_out), (1, down_out)):
        for part in range(4):
            left = SPAN * part
            width = min(SPAN, HIDDEN - left)
            target[:, left : left + width] = gathered[which, part].astype(F32)[:WIDTH, :width]


def result_call(*operands):
    vmem = pl.BlockSpec(memory_space=pltpu.VMEM)
    return pl.pallas_call(
        result_kernel,
        out_shape=[
            jax.ShapeDtypeStruct((LEVELS * ROWS, COLS), F32),
            jax.ShapeDtypeStruct((WIDTH, HIDDEN), F32),
            jax.ShapeDtypeStruct((WIDTH, HIDDEN), F32),
            jax.ShapeDtypeStruct((7, 7, WIDTH), F32),
        ],
        in_specs=[vmem] * 3,
        out_specs=[vmem] * 4,
    )(*operands)


def per_device(
    ocean_state, ocean_mask, cotangent, encoder_weight, encoder_bias, depth_weight,
    norm_gain, up_weight, down_weight, decoder_weight,
):
    cells = ROWS * lax.axis_size("lat") * COLS * lax.axis_size("lon")
    pack, spread = edge_tables()
    parts = main_call(
        1.0 / math.sqrt(cells),
        ocean_state.reshape(LEVELS * ROWS, COLS), ocean_mask, cotangent.reshape(LEVELS * ROWS, COLS),
        encoder_weight, encoder_bias[None, :], jnp.transpose(depth_weight, (1, 2, 0)), norm_gain[None, :],
        up_weight.T, down_weight, decoder_weight.T, jnp.asarray(pack), jnp.asarray(spread))
    state_grad, up_sum, down_sum, depth_sum = result_call(*parts)
    return (
        state_grad.reshape(ocean_state.shape),
        up_sum.T,
        down_sum,
        jnp.transpose(depth_sum, (2, 0, 1)),
    )


def solution(mesh):
    return jax.shard_map(
        per_device,
        mesh=mesh,
        in_specs=(
            P(None, "lat", "lon"), P("lat", "lon"), P(None, "lat", "lon"),
            P(), P(), P(), P(), P(), P(), P(),
        ),
        out_specs=(P(None, "lat", "lon"), P(), P(), P()),
        check_vma=False,
    )
```

```python
import functools
import math

import jax
import jax.numpy as jnp
import numpy as np
from jax import lax
from jax.experimental import pallas as pl
from jax.experimental.pallas import tpu as pltpu
from jax.sharding import PartitionSpec as P

EPSILON = 1e-06
GELU_SCALE = 0.7978845608028654
GELU_CUBE = 0.044715
MESH = pl.DeviceIdType.MESH
F32 = jnp.float32
BF16 = jnp.bfloat16
LEVELS = 100
WIDTH = 200
HIDDEN = 800
ROWS = 8
COLS = 128
CHUNKS = 4
SPAN = 256
FULL = 208
BLOCKS = FULL // 16

STEPS = ((-1, 0), (1, 0), (1, 0), (-1, 0), (0, 1), (0, -1), (1, 1), (1, -1), (-1, 1), (-1, -1))
BANDS = ((0, 1, 0, 2), (6, 0, 1, 2), (5, 0, 0, 1), (2, 1, 2, 1))
LINES = {4: (16, 16, 32), 5: (80, 80, 32), 6: (48, 0, 16), 7: (112, 64, 16), 8: (0, 48, 16), 9: (64, 112, 16)}
ORDER = (0, 3, 2, 1)
BAND_OF = {0: 0, 3: 1, 2: 2, 1: 3}
MEETS = tuple((0, x, k, k - x) for x in range(3) for k in range(x, 3)) + tuple(
    (1, x, k, 6 + k - x) for x in range(3) for k in range(x + 1))


def edge_tables():
    pack = np.zeros((ROWS * COLS, 128), np.float32)
    spread = np.zeros((CHUNKS, 128, SPAN), np.float32)
    for side in range(2):
        for k in range(3):
            column = k if side else 125 + k
            for first, step, sent, rows in ((0, 4, 0, 3), (16, 8, 0, 8), (48, 4, 5, 3)):
                for r in range(rows):
                    pack[COLS * (sent + r) + column, 64 * side + first + step * k + r] = 1.0
            for y in range(ROWS):
                column = 125 + k if side else k
                for part in (0, 48):
                    spread[y // 2, part + 24 * side + 8 * k + y, COLS * (y % 2) + column] = 1.0
    return pack.astype(jnp.bfloat16), spread.astype(jnp.bfloat16)


def dot(a, b):
    return jnp.dot(a, b, preferred_element_type=F32)


def dot_nt(a, b):
    return lax.dot_general(a, b, (((1,), (1,)), ((), ())), preferred_element_type=F32)


def gelu_parts(p):
    square = p * p
    half = 0.5 * jnp.tanh(p * (GELU_SCALE + (GELU_SCALE * GELU_CUBE) * square)) + 0.5
    value = p * half
    slope = half + value * (1.0 - half) * (2.0 * GELU_SCALE + (6.0 * GELU_SCALE * GELU_CUBE) * square)
    return value, slope


def rows_of(value):
    return value[:, :COLS], value[:, COLS:]


def pair(ref, k):
    return jnp.concatenate([ref[2 * k], ref[2 * k + 1]], axis=1)


INPUTS = 12
FIRST = (0, 1, 3, 4, 5, 6)


def staged_kernel(scale, *refs):
    raw, rest, buffers, sems = refs[:INPUTS], refs[INPUTS : -INPUTS - 1], refs[-INPUTS - 1 : -1], refs[-1]
    copies = [pltpu.make_async_copy(raw[n], buffers[n], sems.at[n]) for n in range(INPUTS)]

    def start():
        for n in FIRST + tuple(n for n in range(INPUTS) if n not in FIRST):
            copies[n].start()

    def arrive(first):
        for n in range(INPUTS):
            if (n in FIRST) == first:
                copies[n].wait()

    main_kernel(scale, start, arrive, *buffers, *rest)


def main_kernel(
    scale, start, arrive, state, mask, cot, encw, bias_in, depth_in, gain_in, upt, downw, dect, pack, spread,
    out, gathered, depth_out,
    taps, conv, std_one, std_two, inv_one, inv_two,
    act_one, slope_one, normed_one, normed_two, join, grad_mid, depth_acc,
    upw, downt, decw, enct, own, edge_rows, line_out, line_in, send_sem, recv_sem,
    tall, params, sums, half_out, half_in, quarter_out, quarter_in, slot_sum, slot_out, slot_in, slot_done,
    depth_own, depth_got, depth_mid, depth_peer, depth_all, sum_send, sum_recv,
    edges, fix, edge_terms,
):
    start()
    lat, lon = lax.axis_index("lat"), lax.axis_index("lon")
    lats, lons = lax.axis_size("lat"), lax.axis_size("lon")
    has_north, has_south = lat > 0, lat < lats - 1
    north, south = lat - 1, lat + 1
    east, west = lax.rem(lon + 1, lons), lax.rem(lon + lons - 1, lons)
    x_at, core = lat // 4, lax.rem(lat, 2)
    member = lon // 2 * 4 + lax.rem(lon, 2) * 2 + lax.rem(lat // 2, 2)

    def core_peer():
        return (lat + 1 - 2 * core, lon)

    def line_peer(d):
        return (lax.rem(x_at + d, 4) * 4 + lax.rem(lat, 4), lon)

    def chip_peer(d):
        flip, step = d // 4, d % 4
        side = 1 - core if flip else core
        return (lax.rem(x_at + step, 4) * 4 + lax.rem(lat // 2, 2) * 2 + side, lon)

    def member_at(d):
        return lax.rem(member + d, 16)

    def plane_peer(d):
        other = member_at(d)
        z_at, y_at = other // 4, lax.rem(other, 4)
        return (x_at * 4 + lax.rem(y_at, 2) * 2 + core, z_at * 2 + y_at // 2)

    lat_of = {0: lat, 1: south, -1: north}
    lon_of = {0: lon, 1: east, -1: west}

    def when_lat(step, run):
        if step == 0:
            run()
        elif step > 0:
            pl.when(has_south)(run)
        else:
            pl.when(has_north)(run)

    barrier = pltpu.get_barrier_semaphore()
    for step_lat, step_lon in STEPS[2:]:
        when_lat(step_lat, lambda a=step_lat, b=step_lon: pl.semaphore_signal(
            barrier, inc=1, device_id=(lat_of[a], lon_of[b]), device_id_type=MESH))

    for peer in [chip_peer(d) for d in range(1, 8)] + [plane_peer(d) for d in range(1, 16)]:
        pl.semaphore_signal(barrier, inc=1, device_id=peer, device_id_type=MESH)

    def copy_of(turn, m):
        if m < 4:
            first, side, filled, count = BANDS[m]
            src = own.at[turn, pl.ds(first, count)]
            dst = edge_rows.at[turn, side, pl.ds(filled, count)]
        else:
            first, filled, count = LINES[m]
            src, dst = line_out.at[turn, pl.ds(first, count)], line_in.at[turn, pl.ds(filled, count)]
        return pltpu.make_async_remote_copy(
            src_ref=src, dst_ref=dst, send_sem=send_sem.at[turn, m], recv_sem=recv_sem.at[turn, m],
            device_id=(lat_of[STEPS[m][0]], lon_of[STEPS[m][1]]), device_id_type=MESH)

    def send_lines(turn):
        flat = jnp.concatenate([own[turn, r] for r in range(ROWS)], axis=1)
        picked = dot(flat, pack[...])
        picked = jnp.concatenate([picked, jnp.zeros((48, 128), F32)], axis=0)
        line_out[turn] = picked.T.astype(BF16)
        for m in range(4, 10):
            when_lat(STEPS[m][0], lambda m=m: copy_of(turn, m).start())

    def take_rows(turn):
        for m in range(4):
            when_lat(-STEPS[m][0], lambda m=m: copy_of(turn, m).wait_recv())

    def take_lines(turn, slot, adjoint):
        for m in range(4, 10):
            when_lat(-STEPS[m][0], lambda m=m: copy_of(turn, m).wait_recv())
        lines = line_in[turn].astype(F32)
        for side in range(2):
            for k in range(3):
                base, at = 64 * side, 3 * side + k
                edges[slot, at, 0:3] = lines[base + 4 * k : base + 4 * k + 3]
                edges[slot, at, 3:11] = lines[base + 16 + 8 * k : base + 24 + 8 * k]
                edges[slot, at, 11:14] = lines[base + 48 + 4 * k : base + 51 + 4 * k]
        fixes = [jnp.zeros((8, SPAN), F32)] * 6
        for i in range(7):
            for side, x, k, j in MEETS:
                t = 48 - (7 * i + j) if adjoint else 7 * i + j
                fixes[3 * side + x] = fixes[3 * side + x] + tall[t : t + 1] * edges[slot, 3 * side + k, i : i + 8]
        total = jnp.concatenate(fixes, axis=0)
        coarse = total.astype(BF16).astype(F32)
        fix[...] = jnp.concatenate([coarse, total - coarse, jnp.zeros((32, SPAN), F32)], axis=0).T[:WIDTH].astype(BF16)

    def edge_depth(turn, slot, fresh):
        mine = line_out[turn].astype(F32)
        for i in range(7):
            for j in (0, 1, 2, 4, 5, 6):
                term = jnp.zeros((8, SPAN), F32)
                for side, x, k, at in MEETS:
                    if at == j:
                        base = (16 if side else 80) + 8 * x
                        term = term + mine[base : base + 8] * edges[slot, 3 * side + k, i : i + 8]
                term = jnp.sum(term, axis=0, keepdims=True)
                row = pl.ds(7 * i + j, 1)
                edge_terms[row] = term if fresh else edge_terms[row] + term

    def keep(turn, k, value):
        filled = jnp.concatenate([value, jnp.zeros((8, SPAN), F32)], axis=0).astype(BF16)
        own[turn, 2 * k], own[turn, 2 * k + 1] = rows_of(filled)
        m = BAND_OF[k]
        if turn > 0:
            when_lat(STEPS[m][0], lambda: copy_of(turn, m).start())

    lane = lax.broadcasted_iota(jnp.int32, (1, 16, COLS), 2)
    nothing = jnp.zeros((), BF16)

    def shifted(main, s):
        if s == 0:
            return main
        if s > 0:
            return pltpu.roll(jnp.where(lane < s, nothing, main), COLS - s, 2)
        return pltpu.roll(jnp.where(lane >= COLS + s, nothing, main), -s, 2)

    def tap(i, j, at, adjoint):
        return taps[48 - (7 * i + j) if adjoint else 7 * i + j, at, :][None]

    def over_blocks(body, first_block, last_block):
        def block(b, carry):
            body(pl.ds(pl.multiple_of(16 * b, 16), 16))
            return carry
        lax.fori_loop(first_block, last_block, block, 0, unroll=3 if last_block - first_block > 4 else 1)

    def depthwise(turn, adjoint, first_block=0, last_block=BLOCKS):
        def block(at):
            main = own[turn, :, at, :]
            total = None
            for j in range(7):
                moved = shifted(main, j - 3)
                part = None
                for i in (3, 0, 1, 2, 4, 5, 6):
                    low, high = max(0, 3 - i), min(8, 11 - i)
                    term = tap(i, j, at, adjoint) * moved[low + i - 3 : high + i - 3]
                    if part is None:
                        part = term
                        continue
                    pieces = [part[:low]] if low else []
                    pieces.append(part[low:high] + term)
                    pieces += [part[high:]] if high < 8 else []
                    part = jnp.concatenate(pieces, axis=0)
                part = part.astype(F32)
                total = part if total is None else total + part
            conv[:, at, :] = total
        over_blocks(block, first_block, last_block)

    def depthwise_ends(turn, adjoint):
        def block(at):
            top, bottom = edge_rows[turn, 0, :, at, :], edge_rows[turn, 1, :, at, :]
            high, low = conv[0:3, at, :], conv[5:8, at, :]
            for j in range(7):
                above, below = shifted(top, j - 3), shifted(bottom, j - 3)
                over, under = [None] * 3, [None] * 3
                for i in range(3):
                    weight, mirror = tap(i, j, at, adjoint), tap(6 - i, j, at, adjoint)
                    for y in range(3 - i):
                        term = weight * above[y + i : y + i + 1]
                        over[y] = term if over[y] is None else over[y] + term
                        term = mirror * below[2 - y - i : 3 - y - i]
                        under[2 - y] = term if under[2 - y] is None else under[2 - y] + term
                high = high + jnp.concatenate(over, axis=0).astype(F32)
                low = low + jnp.concatenate(under, axis=0).astype(F32)
            conv[0:3, at, :] = high
            conv[5:8, at, :] = low
        over_blocks(block, 0, BLOCKS)

    def depth_terms(turn, upper, fresh, first_block=0, last_block=BLOCKS):
        def block(at):
            main = jnp.concatenate(
                [edge_rows[turn, 0, :, at, :], own[turn, :, at, :], edge_rows[turn, 1, :, at, :]], axis=0)
            slope = own[upper, :, at, :]
            for j in range(7):
                moved = shifted(main, j - 3)
                for i in range(7):
                    product = slope * moved[i : i + ROWS]
                    term = product[0]
                    for y in range(1, ROWS):
                        term = term + product[y]
                    term = term.astype(F32)
                    if fresh:
                        depth_acc[7 * i + j, at, :] = term
                    else:
                        depth_acc[7 * i + j, at, :] += term
        over_blocks(block, first_block, last_block)

    def whole(k):
        return pair(conv, k)[:WIDTH] + dot(fix[...], spread[k])

    def over_chunks(body):
        for k in ORDER:
            body(k)

    def mask_of(k):
        both = jnp.concatenate([mask[pl.ds(2 * k, 1), :], mask[pl.ds(2 * k + 1, 1), :]], axis=1)
        return both.astype(F32)

    def levels_of(ref, k):
        return jnp.concatenate(
            [ref[pl.ds(2 * k + q, LEVELS, stride=ROWS), :] for q in range(2)], axis=1)

    arrive(True)
    tall[...] = jnp.zeros_like(tall)
    for i in range(7):
        tall[7 * i : 7 * i + 7, :WIDTH] = depth_in[i]
    tall[49:50, :WIDTH] = bias_in[...]
    tall[50:51, :WIDTH] = gain_in[...]
    params[...] = tall[...].T[:FULL]
    bias = params[:WIDTH, 49:50]
    gain = params[:WIDTH, 50:51]

    def encode(k, value, turn):
        keep(turn, k, dot(encw[...], value.astype(BF16)) + bias)

    over_chunks(lambda k: encode(k, levels_of(state, k), 0))

    def ends(turn):
        @pl.when(jnp.logical_not(has_north))
        def _():
            edge_rows[turn, 0] = jnp.zeros_like(edge_rows[turn, 0])
            for part in (0, 64):
                line_in[turn, pl.ds(part, 16)] = jnp.zeros((16, SPAN), BF16)

        @pl.when(jnp.logical_not(has_south))
        def _():
            edge_rows[turn, 1] = jnp.zeros_like(edge_rows[turn, 1])
            for part in (48, 112):
                line_in[turn, pl.ds(part, 16)] = jnp.zeros((16, SPAN), BF16)

    arrive(False)
    peers = 24 + 3 * jnp.minimum(lat, 1) + 3 * jnp.minimum(lats - 1 - lat, 1)
    pl.semaphore_wait(barrier, peers)
    for m in range(4):
        when_lat(STEPS[m][0], lambda m=m: copy_of(0, m).start())
    send_lines(0)

    for turn in range(4):
        ends(turn)
    for t in range(49):
        taps[t] = jnp.broadcast_to(params[:, t : t + 1], (FULL, COLS)).astype(BF16)
    upw[...] = upt[...].astype(F32).T.astype(BF16)
    sums[...] = jnp.zeros_like(sums)
    edge_terms[...] = jnp.zeros_like(edge_terms)
    downt[...] = downw[...].astype(F32).T.astype(BF16)
    decw[...] = dect[...].astype(F32).T.astype(BF16)
    enct[...] = encw[...].astype(F32).T.astype(BF16)

    depthwise(0, False)
    take_rows(0)
    depthwise_ends(0, False)
    take_lines(0, 0, False)

    def normalize(k, std, inv, normed):
        value = whole(k)
        centre = value - jnp.sum(value, axis=0, keepdims=True) * (1.0 / WIDTH)
        inverse = lax.rsqrt(jnp.sum(centre * centre, axis=0, keepdims=True) * (1.0 / WIDTH) + EPSILON)
        standard = centre * inverse
        std[2 * k], std[2 * k + 1] = rows_of(standard)
        inv[k] = jnp.broadcast_to(inverse, (8, SPAN))
        result = (standard * gain).astype(BF16)
        normed[k] = result
        return result

    def forward(k):
        ocean = mask_of(k)
        preact = dot(upw[...], normalize(k, std_one, inv_one, normed_one))
        value, slope = gelu_parts(preact)
        value = value.astype(BF16)
        act_one[k] = value
        slope_one[k] = slope.astype(BF16)
        features = pair(own.at[0], k).astype(F32)[:WIDTH]
        joined = (features + ocean * dot(downw[...], value)).astype(BF16)
        middle = levels_of(state, k) + ocean * dot(decw[...], joined)
        encode(k, middle, 1)

    over_chunks(forward)
    send_lines(1)
    depthwise(1, False)
    take_rows(1)
    depthwise_ends(1, False)
    take_lines(1, 1, False)

    def reverse(k, turn, upstream, normed, value, slope, std, inv):
        ocean = mask_of(k)
        grad_join = dot(dect[...], (ocean * upstream).astype(BF16))
        join[k] = grad_join
        grad_branch = (ocean * grad_join).astype(BF16)
        grad_pre = (dot(downt[...], grad_branch) * slope).astype(BF16)
        grad_norm = dot(upt[...], grad_pre)
        standard = pair(std, k)
        grad_hat = grad_norm * gain
        first = jnp.sum(grad_hat, axis=0, keepdims=True) * (1.0 / WIDTH)
        second = jnp.sum(grad_hat * standard, axis=0, keepdims=True) * (1.0 / WIDTH)
        result = inv[k][0:1] * (grad_hat - first - standard * second)
        keep(turn, k, result)
        for which, term in ((0, dot_nt(normed, grad_pre)), (1, dot_nt(grad_branch, value))):
            for part in range(3):
                sums[which, part, :WIDTH, :] += term[:, SPAN * part : SPAN * (part + 1)]
            sums[which, 3, :WIDTH, : HIDDEN - 3 * SPAN] += term[:, 3 * SPAN :]

    def late(k):
        normed = normalize(k, std_two, inv_two, normed_two)
        value, slope = gelu_parts(dot(upw[...], normed))
        reverse(k, 2, levels_of(cot, k), normed, value.astype(BF16), slope, std_two, inv_two)

    over_chunks(late)
    send_lines(2)
    depth_terms(1, 2, True)
    edge_depth(2, 1, True)
    depthwise(2, True)
    take_rows(2)
    depthwise_ends(2, True)
    take_lines(2, 2, True)

    def early(k):
        grad_input = (join[k] + whole(k)).astype(BF16)
        upstream = levels_of(cot, k) + dot(enct[...], grad_input)
        grad_mid[k] = upstream
        reverse(k, 3, upstream, normed_one[k], act_one[k], slope_one[k].astype(F32), std_one, inv_one)

    over_chunks(early)
    send_lines(3)

    def remote(src, dst, slot, peer):
        return pltpu.make_async_remote_copy(
            src_ref=src, dst_ref=dst, send_sem=sum_send.at[slot], recv_sem=sum_recv.at[slot],
            device_id=peer, device_id_type=MESH)

    def line_at(d):
        return lax.rem(x_at + d, 4)

    mine = pl.ds(pl.multiple_of(16 * jnp.minimum(member, 12), 16), 16)
    halves = [remote(half_out.at[line_at(d)], half_in.at[line_at(d)], 75 + d, core_peer()) for d in range(4)]
    backs = [remote(gathered.at[core, line_at(d)], gathered.at[core, line_at(d)], 79 + d, core_peer()) for d in range(4)]
    quarters = [remote(quarter_out.at[line_at(d)], quarter_in.at[d - 1], d, line_peer(d)) for d in range(1, 4)]

    def slot_copy(d):
        other = jnp.minimum(member_at(d), 12)
        rows = pl.ds(pl.multiple_of(16 * other, 16), 16)
        return remote(slot_out.at[rows], slot_in.at[d - 1], 3 + d, plane_peer(d))

    def done_copy(d):
        return remote(slot_done, gathered.at[core, x_at, mine], 18 + d, plane_peer(d))

    def line_copy(d):
        return remote(gathered.at[core, x_at], gathered.at[core, x_at], 33 + d, line_peer(d))

    def depth_copy(d):
        return remote(depth_own.at[member_at(d)], depth_got.at[d - 1], 37 + d, plane_peer(d))

    def peer_copy(d):
        return remote(depth_mid, depth_peer.at[d - 1], 52 + d, chip_peer(d))

    def spread_copy(d):
        return remote(depth_all.at[member], depth_all.at[member], 59 + d, plane_peer(d))

    def owner(index):
        return lambda run: pl.when(index < 13)(run)

    for d in (2, 1, 3, 0):
        half_out[line_at(d)] = sums[1 - core, line_at(d)].astype(BF16)
        halves[d].start()
    depth_terms(0, 3, False, 0, 3)

    for d in (2, 1, 3):
        halves[d].wait_recv()
        quarter_out[line_at(d)] = (sums[core, line_at(d)] + half_in[line_at(d)].astype(F32)).astype(BF16)
        quarters[d - 1].start()
    halves[0].wait_recv()
    slot_sum[...] = sums[core, x_at] + half_in[x_at].astype(F32)
    depth_terms(0, 3, False, 3, BLOCKS)

    for copy in quarters:
        copy.wait_recv()
    slot_sum[...] = slot_sum[...] + (
        quarter_in[0].astype(F32) + quarter_in[1].astype(F32) + quarter_in[2].astype(F32))
    slot_out[...] = slot_sum[...].astype(BF16)
    for d in range(1, 16):
        owner(member_at(d))(lambda d=d: slot_copy(d).start())

    edge_depth(3, 0, False)
    column = lax.broadcasted_iota(jnp.int32, (FULL, COLS), 1)
    picked = jnp.zeros((FULL, COLS), F32)
    for t in range(49):
        picked = jnp.where(column == t, jnp.sum(depth_acc[t], axis=1, keepdims=True), picked)
    turned = jnp.concatenate([picked, jnp.zeros((48, COLS), F32)], axis=0).T[:64] + edge_terms[...]
    for piece in range(16):
        depth_own[piece] = turned[
            8 * (piece // 2) : 8 * (piece // 2) + 8, COLS * (piece % 2) : COLS * (piece % 2) + COLS]
    for d in range(1, 16):
        depth_copy(d).start()
    depthwise(3, True, 0, 5)

    @pl.when(member < 13)
    def _():
        total = slot_sum[mine, :]
        for d in range(1, 16):
            slot_copy(d).wait_recv()
            total = total + slot_in[d - 1].astype(F32)
        total = (total * scale).astype(BF16)
        slot_done[...] = total
        gathered[core, x_at, mine, :] = total
        for d in range(1, 16):
            done_copy(d).start()

    total = depth_own[member]
    for d in range(1, 16):
        depth_copy(d).wait_recv()
        total = total + depth_got[d - 1]
    depth_mid[...] = total
    for d in range(1, 8):
        peer_copy(d).start()
    depthwise(3, True, 5, BLOCKS)

    for d in range(1, 16):
        owner(member_at(16 - d))(lambda d=d: done_copy(d).wait_recv())
    for d in (2, 1, 3):
        line_copy(d).start()
    backs[0].start()
    total = depth_mid[...]
    for d in range(1, 8):
        peer_copy(d).wait_recv()
        total = total + depth_peer[d - 1]
    depth_all[member] = total * scale
    for d in range(1, 16):
        spread_copy(d).start()
    take_rows(3)
    depthwise_ends(3, True)
    take_lines(3, 2, True)

    def last(k):
        grad_input = (join[k] + whole(k)).astype(BF16)
        result = grad_mid[k] + dot(enct[...], grad_input)
        for q in range(2):
            out[pl.ds(2 * k + q, LEVELS, stride=ROWS), :] = result[:, COLS * q : COLS * (q + 1)]

    over_chunks(last)
    for d in (1, 3, 2):
        line_copy(d).wait_recv()
        backs[4 - d].start()
    for d in range(1, 16):
        spread_copy(d).wait_recv()
    for piece in range(16):
        row, left = 8 * (piece // 2), COLS * (piece % 2)
        width = min(COLS, WIDTH - left)
        for t in range(row, min(row + 8, 49)):
            depth_out[t // 7, t % 7 : t % 7 + 1, left : left + width] = depth_all[piece, t - row : t - row + 1, :width]
    for copy in backs:
        copy.wait_recv()

    for copy in halves + quarters + backs:
        copy.wait_send()
    for d in range(1, 4):
        line_copy(d).wait_send()
    for d in range(1, 8):
        peer_copy(d).wait_send()
    for d in range(1, 16):
        owner(member_at(d))(lambda d=d: slot_copy(d).wait_send())
        owner(member)(lambda d=d: done_copy(d).wait_send())
        depth_copy(d).wait_send()
        spread_copy(d).wait_send()
    for turn in range(4):
        for m in range(10):
            when_lat(STEPS[m][0], lambda m=m: copy_of(turn, m).wait_send())


def main_call(scale, *operands):
    vmem = pl.BlockSpec(memory_space=pltpu.VMEM)
    plane = pltpu.VMEM((ROWS, WIDTH, COLS), F32)
    tile = (8, COLS)
    return pl.pallas_call(
        functools.partial(staged_kernel, scale),
        out_shape=[
            jax.ShapeDtypeStruct((LEVELS * ROWS, COLS), F32),
            jax.ShapeDtypeStruct((2, 4, 208, SPAN), BF16),
            jax.ShapeDtypeStruct((7, 7, WIDTH), F32),
        ],
        in_specs=[pl.BlockSpec(memory_space=pl.ANY)] * len(operands),
        out_specs=[vmem] * 3,
        scratch_shapes=[
            pltpu.VMEM((49, FULL, COLS), BF16),
            pltpu.VMEM((ROWS, FULL, COLS), F32),
            plane, plane,
            pltpu.VMEM((CHUNKS, 8, SPAN), F32),
            pltpu.VMEM((CHUNKS, 8, SPAN), F32),
            pltpu.VMEM((CHUNKS, HIDDEN, SPAN), BF16),
            pltpu.VMEM((CHUNKS, HIDDEN, SPAN), BF16),
            pltpu.VMEM((CHUNKS, WIDTH, SPAN), BF16),
            pltpu.VMEM((CHUNKS, WIDTH, SPAN), BF16),
            pltpu.VMEM((CHUNKS, WIDTH, SPAN), F32),
            pltpu.VMEM((CHUNKS, LEVELS, SPAN), F32),
            pltpu.VMEM((49, FULL, COLS), F32),
            pltpu.VMEM((HIDDEN, WIDTH), BF16),
            pltpu.VMEM((HIDDEN, WIDTH), BF16),
            pltpu.VMEM((LEVELS, WIDTH), BF16),
            pltpu.VMEM((LEVELS, WIDTH), BF16),
            pltpu.VMEM((4, ROWS, 208, COLS), BF16),
            pltpu.VMEM((4, 2, 3, 208, COLS), BF16),
            pltpu.VMEM((4, 128, SPAN), BF16),
            pltpu.VMEM((4, 128, SPAN), BF16),
            pltpu.SemaphoreType.DMA((4, 10)),
            pltpu.SemaphoreType.DMA((4, 10)),
            pltpu.VMEM((128, SPAN), F32),
            pltpu.VMEM((FULL, COLS), F32),
            pltpu.VMEM((2, 4, 208, SPAN), F32),
            pltpu.VMEM((4, 208, SPAN), BF16),
            pltpu.VMEM((4, 208, SPAN), BF16),
            pltpu.VMEM((4, 208, SPAN), BF16),
            pltpu.VMEM((3, 208, SPAN), BF16),
            pltpu.VMEM((208, SPAN), F32),
            pltpu.VMEM((208, SPAN), BF16),
            pltpu.VMEM((15, 16, SPAN), BF16),
            pltpu.VMEM((16, SPAN), BF16),
            pltpu.VMEM((16,) + tile, F32),
            pltpu.VMEM((15,) + tile, F32),
            pltpu.VMEM(tile, F32),
            pltpu.VMEM((7,) + tile, F32),
            pltpu.VMEM((16,) + tile, F32),
            pltpu.SemaphoreType.DMA((83,)),
            pltpu.SemaphoreType.DMA((83,)),
            pltpu.VMEM((3, 6, 16, SPAN), F32),
            pltpu.VMEM((WIDTH, COLS), BF16),
            pltpu.VMEM((64, SPAN), F32),
            *[pltpu.VMEM(value.shape, value.dtype) for value in operands],
            pltpu.SemaphoreType.DMA((INPUTS,)),
        ],
        compiler_params=pltpu.CompilerParams(
            collective_id=0, has_side_effects=True, vmem_limit_bytes=58 * 1024 * 1024),
    )(*operands)


def result_kernel(state, gathered, depth, state_out, up_out, down_out, depth_out):
    state_out[...] = state[...]
    depth_out[...] = depth[...]
    for which, target in ((0, up_out), (1, down_out)):
        for part in range(4):
            left = SPAN * part
            width = min(SPAN, HIDDEN - left)
            target[:, left : left + width] = gathered[which, part].astype(F32)[:WIDTH, :width]


def result_call(*operands):
    vmem = pl.BlockSpec(memory_space=pltpu.VMEM)
    return pl.pallas_call(
        result_kernel,
        out_shape=[
            jax.ShapeDtypeStruct((LEVELS * ROWS, COLS), F32),
            jax.ShapeDtypeStruct((WIDTH, HIDDEN), F32),
            jax.ShapeDtypeStruct((WIDTH, HIDDEN), F32),
            jax.ShapeDtypeStruct((7, 7, WIDTH), F32),
        ],
        in_specs=[vmem] * 3,
        out_specs=[vmem] * 4,
    )(*operands)


def per_device(
    ocean_state, ocean_mask, cotangent, encoder_weight, encoder_bias, depth_weight,
    norm_gain, up_weight, down_weight, decoder_weight,
):
    cells = ROWS * lax.axis_size("lat") * COLS * lax.axis_size("lon")
    pack, spread = edge_tables()
    parts = main_call(
        1.0 / math.sqrt(cells),
        ocean_state.reshape(LEVELS * ROWS, COLS), ocean_mask, cotangent.reshape(LEVELS * ROWS, COLS),
        encoder_weight, encoder_bias[None, :], jnp.transpose(depth_weight, (1, 2, 0)), norm_gain[None, :],
        up_weight.T, down_weight, decoder_weight.T, jnp.asarray(pack), jnp.asarray(spread))
    state_grad, up_sum, down_sum, depth_sum = result_call(*parts)
    return (
        state_grad.reshape(ocean_state.shape),
        up_sum.T,
        down_sum,
        jnp.transpose(depth_sum, (2, 0, 1)),
    )


def solution(mesh):
    return jax.shard_map(
        per_device,
        mesh=mesh,
        in_specs=(
            P(None, "lat", "lon"), P("lat", "lon"), P(None, "lat", "lon"),
            P(), P(), P(), P(), P(), P(), P(),
        ),
        out_specs=(P(None, "lat", "lon"), P(), P(), P()),
        check_vma=False,
    )
```
